32 devices in a mesh: sh: 4 (over z), sw: 4 (over y, core), tp: 2 (over x).
Axes of the slice: x: 2, y: 2, z: 4, core: 2. Of those that a mesh axis runs over, the one named last changes fastest.
Arguments:
- queries: bfloat16 [2, 32, 32, 1536], P('tp', 'sh', 'sw'), may hold values from -6 to 6
- keys: bfloat16 [2, 32, 32, 1536], P('tp', 'sh', 'sw'), may hold values from -6 to 6
- values: bfloat16 [2, 32, 32, 1536], P('tp', 'sh', 'sw'), may hold values from -6 to 6
- attn_out: bfloat16 [2, 32, 32, 1536], P('tp', 'sh', 'sw'), may hold values from -6 to 6
- attn_grad: bfloat16 [2, 32, 32, 1536], P('tp', 'sh', 'sw'), may hold values from -192 to 192
- log_sum: float32 [2, 32, 32, 12], P('tp', 'sh', 'sw'), may hold values from 6.1 to 6.9
- window_dirs: int32 [12, 4], replicated, may hold values from 0 to 7, as said below
Outputs:
- q_grad: bfloat16 [2, 32, 32, 1536], P('tp', 'sh', 'sw')
- k_grad: bfloat16 [2, 32, 32, 1536], P('tp', 'sh', 'sw')
- v_grad: bfloat16 [2, 32, 32, 1536], P('tp', 'sh', 'sw')
The draws below stay inside these ranges and needn't reach their ends.
Inputs may be any that keep to these rules, and one draw needn't show every extreme that they name: `window_dirs`: each row names 4 different directions. Within each run of 6 consecutive heads (those of one index of tp) every direction is named by exactly half of the rows.
All inputs are finite; a program needn't handle non-finite values.
Results may differ from the reference program's by a relative error of at most 0.0056.
Values may be sent and summed in bfloat16 or wider, within the bound.
A program may use at most 64 MiB of HBM per device.

```python
import jax
import jax.numpy as jnp
from jax import lax

FRAMES = 2
TILE_H = 8
TILE_W = 8
HD = 128
HEADS_DEV = 6
HEADS = 12
HEIGHT = 32
WIDTH = 32
COLS = 1536
N_SH = 4
N_SW = 4


def draw_window_dirs(key, part):
    slot_ids = jnp.arange(4 * HEADS_DEV, dtype=jnp.int32)
    base_dirs = ((slot_ids + slot_ids // 8) % 8).reshape(HEADS_DEV, 4)
    groups = []
    for group_id in range(HEADS // HEADS_DEV):
        dir_order = jax.random.permutation(jax.random.fold_in(key, 2 * group_id), 8).astype(jnp.int32)
        head_order = jax.random.permutation(jax.random.fold_in(key, 2 * group_id + 1), HEADS_DEV).astype(jnp.int32)
        groups.append(dir_order[base_dirs][head_order])
    return jnp.concatenate(groups, axis=0).astype(jnp.int32)


def level_of(stream_key, shape, pieces, least, largest):
    def one(dim, parts):
        heights = jax.random.uniform(jax.random.fold_in(jax.random.fold_in(stream_key, 6), dim), (parts,), jnp.float32, least / len(pieces), largest / len(pieces))
        return jnp.repeat(jnp.exp(heights), shape[dim] // parts).reshape((-1,) + (1,) * (len(shape) - dim - 1))

    level = one(*pieces[0])
    for cut in pieces[1:]:
        level = level * one(*cut)
    return level


def noise(rng, extent, width, limit, shards=(), held_as=jnp.bfloat16):
    values = width * jax.random.normal(rng, extent, jnp.float32)
    if shards:
        values = values * level_of(rng, extent, shards, -0.22, 0.18)
    return jnp.clip(values, -limit, limit).astype(held_as)


def setup_inputs(seed: int = 0) -> dict:
    seeds = jax.random.split(jax.random.key(seed), 8)
    return {
        "queries": noise(seeds[0], (FRAMES, HEIGHT, WIDTH, COLS), 1.0, 6.0, ((0, 2), (1, 4), (2, 4))),
        "keys": noise(seeds[1], (FRAMES, HEIGHT, WIDTH, COLS), 1.0, 6.0, ((0, 2), (1, 4), (2, 4))),
        "values": noise(seeds[2], (FRAMES, HEIGHT, WIDTH, COLS), 1.0, 6.0, ((0, 2), (1, 4), (2, 4))),
        "attn_out": noise(seeds[3], (FRAMES, HEIGHT, WIDTH, COLS), 1.0, 6.0, ((0, 2), (1, 4), (2, 4))),
        "attn_grad": noise(seeds[4], (FRAMES, HEIGHT, WIDTH, COLS), 32.0, 192.0, ((0, 2), (1, 4), (2, 4))),
        "log_sum": jnp.clip(6.1 + 0.8000002 * jax.random.uniform(seeds[5], (FRAMES, HEIGHT, WIDTH, HEADS), jnp.float32) ** level_of(seeds[5], (FRAMES, HEIGHT, WIDTH, HEADS), ((0, 2), (1, 4), (2, 4)), -0.2, 0.2), 6.1, 6.9),
        "window_dirs": draw_window_dirs(jax.random.fold_in(seeds[7], 71), 0),
    }


NEIGHBOURS = ((-1, -1), (-1, 0), (-1, 1), (0, -1), (0, 1), (1, -1), (1, 0), (1, 1))


def rounded(array):
    return lax.optimization_barrier(array.astype(jnp.bfloat16)).astype(jnp.float32)


def reference(queries, keys, values, attn_out, attn_grad, log_sum, window_dirs):
    tile_tok = FRAMES * TILE_H * TILE_W
    score_scale = HD ** -0.5
    row_delta = jnp.sum((attn_grad.astype(jnp.float32) * attn_out.astype(jnp.float32)).reshape(FRAMES, HEIGHT, WIDTH, HEADS, HD), axis=4)

    def head_view(array):
        return array.reshape(FRAMES, N_SH, TILE_H, N_SW, TILE_W, HEADS, HD)

    def stat_view(array):
        return array.reshape(FRAMES, N_SH, TILE_H, N_SW, TILE_W, HEADS)

    q_view = head_view(queries)
    k_view = head_view(keys)
    v_view = head_view(values)
    g_view = head_view(attn_grad)
    lse_view = stat_view(log_sum)
    delta_view = stat_view(row_delta)
    offsets = jnp.array(NEIGHBOURS, dtype=jnp.int32)
    row_steps = offsets[window_dirs, 0]
    col_steps = offsets[window_dirs, 1]
    head_ids = jnp.broadcast_to(jnp.arange(HEADS, dtype=jnp.int32)[:, None], (HEADS, 4))
    ones_col = jnp.ones((HEADS, 1), jnp.float32)

    def own_heads(view, grid_row, grid_col):
        return view[:, grid_row, :, grid_col].reshape(tile_tok, HEADS, HD).astype(jnp.float32)

    def own_stats(view, grid_row, grid_col):
        return view[:, grid_row, :, grid_col].reshape(tile_tok, HEADS).T

    def near_heads(view, rows_at, cols_at):
        return view[:, rows_at, :, cols_at, :, head_ids].reshape(HEADS, 4, tile_tok, HD).astype(jnp.float32)

    def near_stats(view, rows_at, cols_at):
        return view[:, rows_at, :, cols_at, :, head_ids].reshape(HEADS, 4, tile_tok)

    def placed(rows_raw, cols_raw):
        live = (rows_raw >= 0) & (rows_raw < N_SH) & (cols_raw >= 0) & (cols_raw < N_SW)
        return jnp.clip(rows_raw, 0, N_SH - 1), jnp.clip(cols_raw, 0, N_SW - 1), live.astype(jnp.float32)

    def one_tile(tile_index):
        grid_row = tile_index // N_SW
        grid_col = tile_index % N_SW
        q_here = own_heads(q_view, grid_row, grid_col)
        k_here = own_heads(k_view, grid_row, grid_col)
        v_here = own_heads(v_view, grid_row, grid_col)
        g_here = own_heads(g_view, grid_row, grid_col)
        lse_here = own_stats(lse_view, grid_row, grid_col)
        delta_here = own_stats(delta_view, grid_row, grid_col)
        near_row, near_col, live_near = placed(grid_row + row_steps, grid_col + col_steps)
        k_all = jnp.concatenate([jnp.transpose(k_here, (1, 0, 2))[:, None], near_heads(k_view, near_row, near_col)], axis=1)
        v_all = jnp.concatenate([jnp.transpose(v_here, (1, 0, 2))[:, None], near_heads(v_view, near_row, near_col)], axis=1)
        live_all = jnp.concatenate([ones_col, live_near], axis=1)
        scores = score_scale * jnp.einsum("thd,hjsd->htjs", q_here, k_all)
        attn_prob = jnp.exp(scores - lse_here[:, :, None, None]) * live_all[:, None, :, None]
        grad_prob = jnp.einsum("thd,hjsd->htjs", g_here, v_all)
        grad_score = attn_prob * (grad_prob - delta_here[:, :, None, None])
        score_bf = rounded(grad_score)
        q_grad = score_scale * jnp.einsum("htjs,hjsd->thd", score_bf, k_all)
        k_self = score_scale * jnp.einsum("hts,thd->hsd", score_bf[:, :, 0], q_here)
        v_self = jnp.einsum("hts,thd->hsd", rounded(attn_prob[:, :, 0]), g_here)
        far_row, far_col, live_far = placed(grid_row - row_steps, grid_col - col_steps)
        q_far = near_heads(q_view, far_row, far_col)
        g_far = near_heads(g_view, far_row, far_col)
        lse_far = near_stats(lse_view, far_row, far_col)
        delta_far = near_stats(delta_view, far_row, far_col)
        scores_far = score_scale * jnp.einsum("hjtd,shd->hjts", q_far, k_here)
        prob_far = jnp.exp(scores_far - lse_far[:, :, :, None]) * live_far[:, :, None, None]
        grad_far = jnp.einsum("hjtd,shd->hjts", g_far, v_here)
        score_far = prob_far * (grad_far - delta_far[:, :, :, None])
        k_pieces = score_scale * jnp.einsum("hjts,hjtd->hjsd", rounded(score_far), q_far)
        v_pieces = jnp.einsum("hjts,hjtd->hjsd", rounded(prob_far), g_far)
        k_total = k_self + jnp.sum(rounded(k_pieces), axis=1)
        v_total = v_self + jnp.sum(rounded(v_pieces), axis=1)
        q_out = q_grad.astype(jnp.bfloat16).reshape(tile_tok, HEADS * HD)
        k_out = jnp.transpose(k_total, (1, 0, 2)).astype(jnp.bfloat16).reshape(tile_tok, HEADS * HD)
        v_out = jnp.transpose(v_total, (1, 0, 2)).astype(jnp.bfloat16).reshape(tile_tok, HEADS * HD)
        return q_out, k_out, v_out

    q_tiles, k_tiles, v_tiles = lax.map(one_tile, jnp.arange(N_SH * N_SW, dtype=jnp.int32))

    def from_tiles(tiles):
        shaped = tiles.reshape(N_SH, N_SW, FRAMES, TILE_H, TILE_W, HEADS * HD)
        return jnp.transpose(shaped, (2, 0, 3, 1, 4, 5)).reshape(FRAMES, HEIGHT, WIDTH, HEADS * HD)

    return (from_tiles(q_tiles), from_tiles(k_tiles), from_tiles(v_tiles))
```

```python
import functools

import jax
import jax.numpy as jnp
from jax import lax
from jax.experimental import pallas as pl
from jax.experimental.pallas import tpu as pltpu
from jax.sharding import PartitionSpec as P

E_OF = (1, 7, 4, 0, 3, 2, 8, 5)
BF = jnp.bfloat16
F32 = jnp.float32
NT = (((1,), (1,)), ((), ()))
TN = (((0,), (0,)), ((), ()))


SIDES = (0, 1, 2, 3, 4, 5, 7, 8)
ROW_STEP = (0, -1, 1)
COL_STEP = (-1, 1, 0)


def kernel(
    n_sh, n_sw, half, hd,
    q_in, k_in, v_in, g_in, o_in, lse_in, wd_in,
    dq_out, dk_out, dv_out,
    kv0, kv1, qg, pieces0, pieces1, packed, stats,
    q_ref, k_ref, v_ref, g_ref, o_ref, lse_ref, wd_ref, in_sem,
    dqp, dqs, dqr0, dqr1, own_kv, own_q, xsend, xback,
    head_of, src_of, flat_of, e_of,
    zs, zr, zts, ztr, xs, xr, ws, wr, wts, wtr, bs, br, rxs, rxr, *zbs,
):
    row = lax.axis_index("sh")
    col = lax.axis_index("sw")
    part = lax.axis_index("tp")
    kv = (kv0, kv1)
    pieces = (pieces0, pieces1)
    dqr = (dqr0, dqr1)
    third = half // 2
    zb = [[zbs[(run * 2 + i) * third:(run * 2 + i + 1) * third] for i in (0, 1)] for run in (0, 1)]
    tok = q_ref.shape[0]
    arguments = (
        (q_in, q_ref), (g_in, g_ref), (k_in, k_ref), (v_in, v_ref), (wd_in, wd_ref), (o_in, o_ref), (lse_in, lse_ref),
    )
    loads = [pltpu.make_async_copy(src, dst, in_sem.at[i]) for i, (src, dst) in enumerate(arguments)]
    for load in loads:
        load.start()
    scale = hd ** -0.5
    row_ok = lambda step: (row + step >= 0) & (row + step < n_sh)
    col_ok = lambda step: (col + step >= 0) & (col + step < n_sw)
    spans = [(0, half - third + 1)] + [(half - third + k, half - third + k + 1) for k in range(1, third)]
    MESH = pl.DeviceIdType.MESH

    def sent_to(e):
        return row_ok(ROW_STEP[e % 3]) & col_ok(COL_STEP[e // 3])

    def came_from(e):
        return row_ok(-ROW_STEP[e % 3]) & col_ok(-COL_STEP[e // 3])

    def remote(src, dst, ssem, rsem, device):
        return pltpu.make_async_remote_copy(
            src_ref=src, dst_ref=dst, send_sem=ssem, recv_sem=rsem, device_id=device, device_id_type=MESH,
        )

    def copy_z(run, i, k):
        lo, hi = spans[k]
        return remote(
            qg.at[run, lo:hi], zb[run][i][k], zs.at[run, i, k], zr.at[run, i, k], {"sh": row + 2 * i - 1},
        )

    def copy_zstat(i):
        return remote(stats.at[6], stats.at[7 + i], zts.at[i], ztr.at[i], {"sh": row + 2 * i - 1})

    def copy_x(run):
        src = kv[run].at[:, :, pl.ds(0, tok)]
        dst = kv[run].at[:, :, pl.ds(tok, tok)]
        return remote(src, dst, xs.at[run], xr.at[run], {"tp": 1 - part})

    def copy_w(run, e, k):
        span = pl.ds(k, 1) if e % 3 else pl.ds(0, third)
        at = pl.ds(e * third + k, 1) if e % 3 else pl.ds(e * third, third)
        return remote(
            packed.at[run, e, span], pieces[run].at[at], ws.at[run, e, k], wr.at[run, e, k], {"sw": col + COL_STEP[e // 3]},
        )

    def copy_wstat(e):
        return remote(stats.at[6 + e % 3], stats.at[e], wts.at[e], wtr.at[e], {"sw": col + COL_STEP[e // 3]})

    def copy_back(run, e, k):
        at = run * 9 + e
        home = {"sh": row - ROW_STEP[e % 3], "sw": col - COL_STEP[e // 3]}
        return remote(dqs.at[at, k], dqr[run].at[e * third + k], bs.at[run, e, k], br.at[run, e, k], home)

    def copy_xback(run, k):
        lo, hi = spans[k]
        return remote(xsend.at[run, lo:hi], xback.at[run, lo:hi], rxs.at[run, k], rxr.at[run, k], {"tp": 1 - part})

    barrier = pltpu.get_barrier_semaphore()
    pl.semaphore_signal(barrier, inc=1, device_id={"tp": 1 - part}, device_id_type=MESH)
    count = 1
    for e in SIDES:
        @pl.when(sent_to(e))
        def _():
            near = {"sh": row + ROW_STEP[e % 3], "sw": col + COL_STEP[e // 3]}
            pl.semaphore_signal(barrier, inc=1, device_id=near, device_id_type=MESH)
        count = count + sent_to(e).astype(jnp.int32)

    loads[0].wait()
    loads[1].wait()
    for run in (0, 1):
        for h in range(half):
            cols = slice((run * half + h) * hd, (run * half + h + 1) * hd)
            qg[run, h, 0] = q_ref[:, cols]
            qg[run, h, 1] = g_ref[:, cols]
    pl.semaphore_wait(barrier, count)

    def send_z(run):
        for k in range(third):
            for i in (0, 1):
                @pl.when(row_ok(2 * i - 1))
                def _():
                    copy_z(run, i, k).start()

    send_z(0)
    loads[2].wait()
    loads[3].wait()
    for run in (0, 1):
        for h in range(half):
            cols = slice((run * half + h) * hd, (run * half + h + 1) * hd)
            kv[run][0, h, :tok] = k_ref[:, cols]
            kv[run][1, h, :tok] = v_ref[:, cols]
        copy_x(run).start()

    loads[4].wait()
    for run in (0, 1):
        dirs = [[wd_ref[j, run * half + h] for j in range(4)] for h in range(half)]
        flat = [[jnp.int32(0) for j in range(4)] for h in range(half)]
        tile = [[jnp.int32(0) for j in range(4)] for h in range(half)]
        for d in range(8):
            e = E_OF[d]
            seen = jnp.int32(0)
            heads = [jnp.int32(0) for _ in range(third)]
            srcs = [jnp.int32(0) for _ in range(third)]
            for h in range(half):
                named = [(dirs[h][j] == d).astype(jnp.int32) for j in range(4)]
                member = jnp.minimum(named[0] + named[1] + named[2] + named[3], 1)
                slot = jnp.minimum(named[1] + 2 * named[2] + 3 * named[3], 3) + (run * half + h) * 4
                at = e * third + jnp.minimum(seen, third - 1)
                for j in range(4):
                    flat[h][j] = flat[h][j] + named[j] * at
                    tile[h][j] = tile[h][j] + named[j] * e
                for s in range(third):
                    mine = member * (seen == s).astype(jnp.int32)
                    heads[s] = heads[s] + mine * h
                    srcs[s] = srcs[s] + mine * slot
                seen = seen + member
            for s in range(third):
                head_of[(run * 9 + e) * third + s] = heads[s]
                src_of[(run * 9 + e) * third + s] = srcs[s]
        for h in range(half):
            for j in range(4):
                flat_of[(run * half + h) * 4 + j] = flat[h][j]
                e_of[(run * half + h) * 4 + j] = tile[h][j]

    def pack(run, e, s):
        i = e % 3
        h = head_of[(run * 9 + e) * third + s]
        if i == 0:
            block = qg[run, h]
        else:
            held = zb[run][i - 1]
            block = held[0][jnp.minimum(h, spans[0][1] - 1)]
            for k in range(1, s + 1):
                block = jnp.where(h == spans[k][0], held[k][0], block)
        if e // 3 == 2:
            pieces[run][e * third + s] = block
        else:
            packed[run, e, s] = block

    for run in (0, 1):
        for e in (0, 3):
            @pl.when(sent_to(e))
            def _():
                for s in range(third):
                    pack(run, e, s)
                copy_w(run, e, 0).start()

    loads[5].wait()
    loads[6].wait()
    lane = lax.broadcasted_iota(jnp.int32, (tok, hd), 1)
    table = jnp.zeros((tok, hd), F32)
    for at in range(2 * half):
        cols = slice(at * hd, (at + 1) * hd)
        delta = jnp.sum(g_ref[:, cols].astype(F32) * o_ref[:, cols].astype(F32), axis=1, keepdims=True)
        table = jnp.where(lane == at, lse_ref[:, at:at + 1], table)
        table = jnp.where(lane == 16 + at, delta, table)
    turned = jnp.concatenate([table, jnp.zeros((hd - tok, hd), F32)], axis=0).T
    stats[6] = turned[:16] + pltpu.roll(turned[16:32], tok, 1)
    for i in (0, 1):
        @pl.when(row_ok(2 * i - 1))
        def _():
            copy_zstat(i).start()
    for e in (0, 3):
        @pl.when(sent_to(e))
        def _():
            copy_wstat(e).start()
    send_z(1)

    for e in SIDES:
        @pl.when(jnp.logical_not(came_from(e)))
        def _():
            stats[e] = jnp.zeros(stats.shape[1:], F32)
            for run in (0, 1):
                pieces[run][e * third:(e + 1) * third] = jnp.zeros((third,) + pieces0.shape[1:], BF)

        @pl.when(jnp.logical_not(sent_to(e)))
        def _():
            for run in (0, 1):
                dqr[run][e * third:(e + 1) * third] = jnp.zeros((third,) + dqr0.shape[1:], BF)

    def relay(run, k):
        for i in (1, 2):
            @pl.when(row_ok(-ROW_STEP[i]))
            def _():
                copy_z(run, i - 1, k).wait_recv()
                if run == 0 and k == third - 1:
                    copy_zstat(i - 1).wait_recv()
                for e in (i, 3 + i):
                    @pl.when(col_ok(COL_STEP[e // 3]))
                    def _():
                        pack(run, e, k)
                        copy_w(run, e, k).start()
                        if run == 0 and k == third - 1:
                            copy_wstat(e).start()
                pack(run, 6 + i, k)

    def products(keys, vals, q, g, lse, delta):
        scores = lax.dot_general(keys, q, NT, preferred_element_type=F32)
        prob = jnp.exp(scores * scale - lse)
        grad_prob = lax.dot_general(vals, g, NT, preferred_element_type=F32)
        score_bf = (prob * (grad_prob - delta)).astype(BF)
        dv = jnp.dot(prob.astype(BF), g, preferred_element_type=F32)
        dk = jnp.dot(score_bf, q, preferred_element_type=F32) * scale
        dq = lax.dot_general(score_bf, keys, TN, preferred_element_type=F32) * scale
        return dq, dk, dv

    def own(run):
        for h in range(half):
            at = run * half + h
            stat = stats[6, at:at + 1, :]
            dq, dk, dv = products(
                kv[run][0, h], kv[run][1, h], qg[run, h, 0], qg[run, h, 1], stat[:, :tok], pltpu.roll(stat, tok, 1)[:, :tok],
            )
            own_q[at] = dq
            own_kv[at, 0] = dk
            own_kv[at, 1] = dv

    first = lax.broadcasted_iota(jnp.int32, (1, hd), 1) < tok

    def near(run, h):
        at = run * half + h
        where = [flat_of[at * 4 + j] for j in range(4)]
        q = jnp.concatenate([pieces[run][w, 0] for w in where], axis=0)
        g = jnp.concatenate([pieces[run][w, 1] for w in where], axis=0)
        stat = [stats[e_of[at * 4 + j], at:at + 1, :] for j in range(4)]
        turn = [pltpu.roll(s, tok, 1) for s in stat]
        lse = jnp.concatenate([jnp.where(first, stat[j], turn[j + 1]) for j in (0, 2)], axis=1)
        delta = jnp.concatenate([jnp.where(first, turn[j], stat[j + 1]) for j in (0, 2)], axis=1)
        dq, dk, dv = products(kv[run][0, h], kv[run][1, h], q, g, lse, delta)
        for j in range(4):
            dqp[at * 4 + j] = dq[j * tok:(j + 1) * tok].astype(BF)
        for a, grad in ((0, dk), (1, dv)):
            total = own_kv[at, a] + grad
            own_kv[at, a, :tok] = total[:tok]
            xsend[run, h, a] = total[tok:].astype(BF)

    def arrived(run):
        for e in range(6):
            @pl.when(came_from(e))
            def _():
                for k in range(third if e % 3 else 1):
                    copy_w(run, e, k).wait_recv()
                if run == 0:
                    copy_wstat(e).wait_recv()

    def batch(run, k):
        for h in range(*spans[k]):
            near(run, h)
        copy_xback(run, k).start()
        for e in SIDES:
            dqs[run * 9 + e, k] = dqp[src_of[(run * 9 + e) * third + k]]

            @pl.when(came_from(e))
            def _():
                copy_back(run, e, k).start()

    def finish_kv(run, k):
        copy_xback(run, k).wait_recv()
        for h in range(*spans[k]):
            cols = slice((run * half + h) * hd, (run * half + h + 1) * hd)
            for a, out in ((0, dk_out), (1, dv_out)):
                out[:, cols] = (own_kv[run * half + h, a, :tok] + xback[run, h, a].astype(F32)).astype(BF)

    def finish_q(run):
        for e in SIDES:
            @pl.when(sent_to(e))
            def _():
                for k in range(third):
                    copy_back(run, e, k).wait_recv()
        for h in range(half):
            at = run * half + h
            total = own_q[at]
            for j in range(4):
                total = total + dqr[run][flat_of[at * 4 + j]].astype(F32)
            dq_out[:, at * hd:(at + 1) * hd] = total.astype(BF)

    for k in range(third):
        relay(0, k)
    copy_x(0).wait_recv()
    own(0)
    relay(1, 0)
    arrived(0)
    for k in range(third):
        batch(0, k)
    for k in range(1, third):
        relay(1, k)
    copy_x(1).wait_recv()
    own(1)
    arrived(1)
    for k in range(third):
        batch(1, k)
    for k in range(third):
        finish_kv(0, k)
    finish_q(0)
    for k in range(third):
        finish_kv(1, k)
    finish_q(1)
    for run in (0, 1):
        copy_x(run).wait_send()
        for k in range(third):
            copy_xback(run, k).wait_send()
            for i in (0, 1):
                @pl.when(row_ok(2 * i - 1))
                def _():
                    copy_z(run, i, k).wait_send()
                    if run == 0 and k == 0:
                        copy_zstat(i).wait_send()
            for e in range(6):
                @pl.when(row_ok(-ROW_STEP[e % 3]) & col_ok(COL_STEP[e // 3]))
                def _():
                    if e % 3 or k == 0:
                        copy_w(run, e, k).wait_send()
                    if run == 0 and k == 0:
                        copy_wstat(e).wait_send()
            for e in SIDES:
                @pl.when(came_from(e))
                def _():
                    copy_back(run, e, k).wait_send()


def hand_out(a_in, b_in, c_in, a_out, b_out, c_out, held, in_sem, out_sem):
    ins = [pltpu.make_async_copy(src, held.at[i], in_sem.at[i]) for i, src in enumerate((a_in, b_in, c_in))]
    outs = [pltpu.make_async_copy(held.at[i], dst, out_sem.at[i]) for i, dst in enumerate((a_out, b_out, c_out))]
    for copy in ins:
        copy.start()
    for first, second in zip(ins, outs):
        first.wait()
        second.start()
    for copy in outs:
        copy.wait()


def local(n_sh, n_sw, queries, keys, values, attn_out, attn_grad, log_sum, window_dirs):
    shape = queries.shape
    tok = shape[0] * shape[1] * shape[2]
    cols = shape[3]
    heads = log_sum.shape[3]
    half = heads // 2
    third = half // 2
    hd = cols // heads
    flat = lambda array: array.reshape(tok, array.shape[3])
    vmem = pl.BlockSpec(memory_space=pltpu.VMEM)
    hbm = pl.BlockSpec(memory_space=pltpu.HBM)
    dma = pltpu.SemaphoreType.DMA
    scratch = (
        [pltpu.VMEM((2, half, 2 * tok, hd), BF) for _ in range(2)]
        + [
            pltpu.VMEM((2, half, 2, tok, hd), BF),
            pltpu.VMEM((9 * third, 2, tok, hd), BF),
            pltpu.VMEM((9 * third, 2, tok, hd), BF),
            pltpu.VMEM((2, 6, third, 2, tok, hd), BF),
            pltpu.VMEM((9, 16, hd), F32),
        ]
        + [pltpu.VMEM((tok, cols), BF) for _ in range(5)]
        + [pltpu.VMEM((tok, heads), F32), pltpu.SMEM((4, heads), jnp.int32), dma((7,))]
        + [
            pltpu.VMEM((heads * 4, tok, hd), BF),
            pltpu.VMEM((18, third, tok, hd), BF),
            pltpu.VMEM((9 * third, tok, hd), BF),
            pltpu.VMEM((9 * third, tok, hd), BF),
            pltpu.VMEM((heads, 2, 2 * tok, hd), F32),
            pltpu.VMEM((heads, tok, hd), F32),
            pltpu.VMEM((2, half, 2, tok, hd), BF),
            pltpu.VMEM((2, half, 2, tok, hd), BF),
            pltpu.SMEM((18 * third,), jnp.int32),
            pltpu.SMEM((18 * third,), jnp.int32),
            pltpu.SMEM((heads * 4,), jnp.int32),
            pltpu.SMEM((heads * 4,), jnp.int32),
        ]
    )
    for sem in ((2, 2, third), (2,), (2,), (2, 6, third), (6,), (2, 9, third), (2, third)):
        scratch += [dma(sem), dma(sem)]
    for _ in range(4):
        scratch += [pltpu.VMEM((half - third + 1 if k == 0 else 1, 2, tok, hd), BF) for k in range(third)]
    dq, dk, dv = pl.pallas_call(
        functools.partial(kernel, n_sh, n_sw, half, hd),
        out_shape=[jax.ShapeDtypeStruct((tok, cols), BF)] * 3,
        in_specs=[hbm] * 7,
        out_specs=[vmem] * 3,
        scratch_shapes=scratch,
        compiler_params=pltpu.CompilerParams(
            collective_id=0, has_side_effects=True, vmem_limit_bytes=64 * 2**20
        ),
    )(flat(queries), flat(keys), flat(values), flat(attn_grad), flat(attn_out), flat(log_sum), window_dirs.T)
    dq, dk, dv = pl.pallas_call(
        hand_out,
        out_shape=[jax.ShapeDtypeStruct((tok, cols), BF)] * 3,
        in_specs=[hbm] * 3,
        out_specs=[hbm] * 3,
        scratch_shapes=[pltpu.VMEM((3, tok, cols), BF), dma((3,)), dma((3,))],
        compiler_params=pltpu.CompilerParams(vmem_limit_bytes=64 * 2**20),
    )(dq, dk, dv)
    return tuple(array.reshape(shape) for array in (dq, dk, dv))


def solution(mesh):
    spec = P("tp", "sh", "sw", None)
    return jax.shard_map(
        functools.partial(local, mesh.shape["sh"], mesh.shape["sw"]),
        mesh=mesh,
        in_specs=(spec,) * 6 + (P(),),
        out_specs=(spec,) * 3,
        check_vma=False,
    )
```

```python
import functools

import jax
import jax.numpy as jnp
from jax import lax
from jax.experimental import pallas as pl
from jax.experimental.pallas import tpu as pltpu
from jax.sharding import PartitionSpec as P

E_OF = (1, 7, 4, 0, 3, 2, 8, 5)
BF = jnp.bfloat16
F32 = jnp.float32
NT = (((1,), (1,)), ((), ()))
TN = (((0,), (0,)), ((), ()))


SIDES = (0, 1, 2, 3, 4, 5, 7, 8)
ROW_STEP = (0, -1, 1)
COL_STEP = (-1, 1, 0)


def kernel(
    n_sh, n_sw, half, hd,
    q_in, k_in, v_in, g_in, o_in, lse_in, wd_in,
    dq_out, dk_out, dv_out,
    kv0, kv1, qg, pieces0, pieces1, packed, stats,
    q_ref, k_ref, v_ref, g_ref, o_ref, lse_ref, wd_ref, in_sem,
    dqp, dqs, dqr0, dqr1, own_kv, own_q, xsend, xback,
    head_of, src_of, flat_of, e_of,
    zs, zr, zts, ztr, xs, xr, ws, wr, wts, wtr, bs, br, rxs, rxr, *zbs,
):
    row = lax.axis_index("sh")
    col = lax.axis_index("sw")
    part = lax.axis_index("tp")
    kv = (kv0, kv1)
    pieces = (pieces0, pieces1)
    dqr = (dqr0, dqr1)
    third = half // 2
    zb = [[zbs[(run * 2 + i) * third:(run * 2 + i + 1) * third] for i in (0, 1)] for run in (0, 1)]
    tok = q_ref.shape[0]
    arguments = (
        (q_in, q_ref), (g_in, g_ref), (k_in, k_ref), (v_in, v_ref), (wd_in, wd_ref), (o_in, o_ref), (lse_in, lse_ref),
    )
    loads = [pltpu.make_async_copy(src, dst, in_sem.at[i]) for i, (src, dst) in enumerate(arguments)]
    for load in loads:
        load.start()
    scale = hd ** -0.5
    row_ok = lambda step: (row + step >= 0) & (row + step < n_sh)
    col_ok = lambda step: (col + step >= 0) & (col + step < n_sw)
    spans = [(0, half - third + 1)] + [(half - third + k, half - third + k + 1) for k in range(1, third)]
    MESH = pl.DeviceIdType.MESH

    def sent_to(e):
        return row_ok(ROW_STEP[e % 3]) & col_ok(COL_STEP[e // 3])

    def came_from(e):
        return row_ok(-ROW_STEP[e % 3]) & col_ok(-COL_STEP[e // 3])

    def remote(src, dst, ssem, rsem, device):
        return pltpu.make_async_remote_copy(
            src_ref=src, dst_ref=dst, send_sem=ssem, recv_sem=rsem, device_id=device, device_id_type=MESH,
        )

    def copy_z(run, i, k):
        lo, hi = spans[k]
        return remote(
            qg.at[run, lo:hi], zb[run][i][k], zs.at[run, i, k], zr.at[run, i, k], {"sh": row + 2 * i - 1},
        )

    def copy_zstat(i):
        return remote(stats.at[6], stats.at[7 + i], zts.at[i], ztr.at[i], {"sh": row + 2 * i - 1})

    def copy_x(run):
        src = kv[run].at[:, :, pl.ds(0, tok)]
        dst = kv[run].at[:, :, pl.ds(tok, tok)]
        return remote(src, dst, xs.at[run], xr.at[run], {"tp": 1 - part})

    def copy_w(run, e, k):
        span = pl.ds(k, 1) if e % 3 else pl.ds(0, third)
        at = pl.ds(e * third + k, 1) if e % 3 else pl.ds(e * third, third)
        return remote(
            packed.at[run, e, span], pieces[run].at[at], ws.at[run, e, k], wr.at[run, e, k], {"sw": col + COL_STEP[e // 3]},
        )

    def copy_wstat(e):
        return remote(stats.at[6 + e % 3], stats.at[e], wts.at[e], wtr.at[e], {"sw": col + COL_STEP[e // 3]})

    def copy_back(run, e, k):
        at = run * 9 + e
        home = {"sh": row - ROW_STEP[e % 3], "sw": col - COL_STEP[e // 3]}
        return remote(dqs.at[at, k], dqr[run].at[e * third + k], bs.at[run, e, k], br.at[run, e, k], home)

    def copy_xback(run, k):
        lo, hi = spans[k]
        return remote(xsend.at[run, lo:hi], xback.at[run, lo:hi], rxs.at[run, k], rxr.at[run, k], {"tp": 1 - part})

    barrier = pltpu.get_barrier_semaphore()
    pl.semaphore_signal(barrier, inc=1, device_id={"tp": 1 - part}, device_id_type=MESH)
    count = 1
    for e in SIDES:
        @pl.when(sent_to(e))
        def _():
            near = {"sh": row + ROW_STEP[e % 3], "sw": col + COL_STEP[e // 3]}
            pl.semaphore_signal(barrier, inc=1, device_id=near, device_id_type=MESH)
        count = count + sent_to(e).astype(jnp.int32)

    loads[0].wait()
    loads[1].wait()
    for run in (0, 1):
        for h in range(half):
            cols = slice((run * half + h) * hd, (run * half + h + 1) * hd)
            qg[run, h, 0] = q_ref[:, cols]
            qg[run, h, 1] = g_ref[:, cols]
    pl.semaphore_wait(barrier, count)

    def send_z(run):
        for k in range(third):
            for i in (0, 1):
                @pl.when(row_ok(2 * i - 1))
                def _():
                    copy_z(run, i, k).start()

    send_z(0)
    loads[2].wait()
    loads[3].wait()
    for run in (0, 1):
        for h in range(half):
            cols = slice((run * half + h) * hd, (run * half + h + 1) * hd)
            kv[run][0, h, :tok] = k_ref[:, cols]
            kv[run][1, h, :tok] = v_ref[:, cols]
        copy_x(run).start()

    loads[4].wait()
    for run in (0, 1):
        dirs = [[wd_ref[j, run * half + h] for j in range(4)] for h in range(half)]
        flat = [[jnp.int32(0) for j in range(4)] for h in range(half)]
        tile = [[jnp.int32(0) for j in range(4)] for h in range(half)]
        for d in range(8):
            e = E_OF[d]
            seen = jnp.int32(0)
            heads = [jnp.int32(0) for _ in range(third)]
            srcs = [jnp.int32(0) for _ in range(third)]
            for h in range(half):
                named = [(dirs[h][j] == d).astype(jnp.int32) for j in range(4)]
                member = jnp.minimum(named[0] + named[1] + named[2] + named[3], 1)
                slot = jnp.minimum(named[1] + 2 * named[2] + 3 * named[3], 3) + (run * half + h) * 4
                at = e * third + jnp.minimum(seen, third - 1)
                for j in range(4):
                    flat[h][j] = flat[h][j] + named[j] * at
                    tile[h][j] = tile[h][j] + named[j] * e
                for s in range(third):
                    mine = member * (seen == s).astype(jnp.int32)
                    heads[s] = heads[s] + mine * h
                    srcs[s] = srcs[s] + mine * slot
                seen = seen + member
            for s in range(third):
                head_of[(run * 9 + e) * third + s] = heads[s]
                src_of[(run * 9 + e) * third + s] = srcs[s]
        for h in range(half):
            for j in range(4):
                flat_of[(run * half + h) * 4 + j] = flat[h][j]
                e_of[(run * half + h) * 4 + j] = tile[h][j]

    def pack(run, e, s):
        i = e % 3
        h = head_of[(run * 9 + e) * third + s]
        if i == 0:
            block = qg[run, h]
        else:
            held = zb[run][i - 1]
            block = held[0][jnp.minimum(h, spans[0][1] - 1)]
            for k in range(1, s + 1):
                block = jnp.where(h == spans[k][0], held[k][0], block)
        if e // 3 == 2:
            pieces[run][e * third + s] = block
        else:
            packed[run, e, s] = block

    for run in (0, 1):
        for e in (0, 3):
            @pl.when(sent_to(e))
            def _():
                for s in range(third):
                    pack(run, e, s)
                copy_w(run, e, 0).start()

    loads[5].wait()
    loads[6].wait()
    lane = lax.broadcasted_iota(jnp.int32, (tok, hd), 1)
    table = jnp.zeros((tok, hd), F32)
    for at in range(2 * half):
        cols = slice(at * hd, (at + 1) * hd)
        delta = jnp.sum(g_ref[:, cols].astype(F32) * o_ref[:, cols].astype(F32), axis=1, keepdims=True)
        table = jnp.where(lane == at, lse_ref[:, at:at + 1], table)
        table = jnp.where(lane == 16 + at, delta, table)
    turned = jnp.concatenate([table, jnp.zeros((hd - tok, hd), F32)], axis=0).T
    stats[6] = turned[:16] + pltpu.roll(turned[16:32], tok, 1)
    for i in (0, 1):
        @pl.when(row_ok(2 * i - 1))
        def _():
            copy_zstat(i).start()
    for e in (0, 3):
        @pl.when(sent_to(e))
        def _():
            copy_wstat(e).start()
    send_z(1)

    for e in SIDES:
        @pl.when(jnp.logical_not(came_from(e)))
        def _():
            stats[e] = jnp.zeros(stats.shape[1:], F32)
            for run in (0, 1):
                pieces[run][e * third:(e + 1) * third] = jnp.zeros((third,) + pieces0.shape[1:], BF)

        @pl.when(jnp.logical_not(sent_to(e)))
        def _():
            for run in (0, 1):
                dqr[run][e * third:(e + 1) * third] = jnp.zeros((third,) + dqr0.shape[1:], BF)

    def relay(run, k):
        for i in (1, 2):
            @pl.when(row_ok(-ROW_STEP[i]))
            def _():
                copy_z(run, i - 1, k).wait_recv()
                if run == 0 and k == third - 1:
                    copy_zstat(i - 1).wait_recv()
                for e in (i, 3 + i):
                    @pl.when(col_ok(COL_STEP[e // 3]))
                    def _():
                        pack(run, e, k)
                        copy_w(run, e, k).start()
                        if run == 0 and k == third - 1:
                            copy_wstat(e).start()
                pack(run, 6 + i, k)

    def products(keys, vals, q, g, lse, delta):
        scores = lax.dot_general(keys, q, NT, preferred_element_type=F32)
        prob = jnp.exp(scores * scale - lse)
        grad_prob = lax.dot_general(vals, g, NT, preferred_element_type=F32)
        score_bf = (prob * (grad_prob - delta)).astype(BF)
        dv = jnp.dot(prob.astype(BF), g, preferred_element_type=F32)
        dk = jnp.dot(score_bf, q, preferred_element_type=F32) * scale
        dq = lax.dot_general(score_bf, keys, TN, preferred_element_type=F32) * scale
        return dq, dk, dv

    def own(run):
        for h in range(half):
            at = run * half + h
            stat = stats[6, at:at + 1, :]
            dq, dk, dv = products(
                kv[run][0, h], kv[run][1, h], qg[run, h, 0], qg[run, h, 1], stat[:, :tok], pltpu.roll(stat, tok, 1)[:, :tok],
            )
            own_q[at] = dq
            own_kv[at, 0] = dk
            own_kv[at, 1] = dv

    first = lax.broadcasted_iota(jnp.int32, (1, hd), 1) < tok

    def near(run, h):
        at = run * half + h
        where = [flat_of[at * 4 + j] for j in range(4)]
        q = jnp.concatenate([pieces[run][w, 0] for w in where], axis=0)
        g = jnp.concatenate([pieces[run][w, 1] for w in where], axis=0)
        stat = [stats[e_of[at * 4 + j], at:at + 1, :] for j in range(4)]
        turn = [pltpu.roll(s, tok, 1) for s in stat]
        lse = jnp.concatenate([jnp.where(first, stat[j], turn[j + 1]) for j in (0, 2)], axis=1)
        delta = jnp.concatenate([jnp.where(first, turn[j], stat[j + 1]) for j in (0, 2)], axis=1)
        dq, dk, dv = products(kv[run][0, h], kv[run][1, h], q, g, lse, delta)
        for j in range(4):
            dqp[at * 4 + j] = dq[j * tok:(j + 1) * tok].astype(BF)
        for a, grad in ((0, dk), (1, dv)):
            total = own_kv[at, a] + grad
            own_kv[at, a, :tok] = total[:tok]
            xsend[run, h, a] = total[tok:].astype(BF)

    def arrived(run):
        for e in range(6):
            @pl.when(came_from(e))
            def _():
                for k in range(third if e % 3 else 1):
                    copy_w(run, e, k).wait_recv()
                if run == 0:
                    copy_wstat(e).wait_recv()

    def batch(run, k):
        for h in range(*spans[k]):
            near(run, h)
        copy_xback(run, k).start()
        for e in SIDES:
            dqs[run * 9 + e, k] = dqp[src_of[(run * 9 + e) * third + k]]

            @pl.when(came_from(e))
            def _():
                copy_back(run, e, k).start()

    def finish_kv(run, k):
        copy_xback(run, k).wait_recv()
        for h in range(*spans[k]):
            cols = slice((run * half + h) * hd, (run * half + h + 1) * hd)
            for a, out in ((0, dk_out), (1, dv_out)):
                out[:, cols] = (own_kv[run * half + h, a, :tok] + xback[run, h, a].astype(F32)).astype(BF)

    def finish_q(run):
        for e in SIDES:
            @pl.when(sent_to(e))
            def _():
                for k in range(third):
                    copy_back(run, e, k).wait_recv()
        for h in range(half):
            at = run * half + h
            total = own_q[at]
            for j in range(4):
                total = total + dqr[run][flat_of[at * 4 + j]].astype(F32)
            dq_out[:, at * hd:(at + 1) * hd] = total.astype(BF)

    for k in range(third):
        relay(0, k)
    copy_x(0).wait_recv()
    own(0)
    relay(1, 0)
    arrived(0)
    for k in range(third):
        batch(0, k)
    for k in range(1, third):
        relay(1, k)
    copy_x(1).wait_recv()
    own(1)
    arrived(1)
    for k in range(third):
        batch(1, k)
    for k in range(third):
        finish_kv(0, k)
    finish_q(0)
    for k in range(third):
        finish_kv(1, k)
    finish_q(1)
    for run in (0, 1):
        copy_x(run).wait_send()
        for k in range(third):
            copy_xback(run, k).wait_send()
            for i in (0, 1):
                @pl.when(row_ok(2 * i - 1))
                def _():
                    copy_z(run, i, k).wait_send()
                    if run == 0 and k == 0:
                        copy_zstat(i).wait_send()
            for e in range(6):
                @pl.when(row_ok(-ROW_STEP[e % 3]) & col_ok(COL_STEP[e // 3]))
                def _():
                    if e % 3 or k == 0:
                        copy_w(run, e, k).wait_send()
                    if run == 0 and k == 0:
                        copy_wstat(e).wait_send()
            for e in SIDES:
                @pl.when(came_from(e))
                def _():
                    copy_back(run, e, k).wait_send()


def hand_out(a_in, b_in, c_in, a_out, b_out, c_out, out_sem):
    outs = [
        pltpu.make_async_copy(src, dst, out_sem.at[i])
        for i, (src, dst) in enumerate(((a_in, a_out), (b_in, b_out), (c_in, c_out)))
    ]
    for copy in outs:
        copy.start()
    for copy in outs:
        copy.wait()


def local(n_sh, n_sw, queries, keys, values, attn_out, attn_grad, log_sum, window_dirs):
    shape = queries.shape
    tok = shape[0] * shape[1] * shape[2]
    cols = shape[3]
    heads = log_sum.shape[3]
    half = heads // 2
    third = half // 2
    hd = cols // heads
    place = pltpu.with_memory_space_constraint
    flat = lambda array: place(array.reshape(tok, array.shape[3]), pltpu.HBM)
    vmem = pl.BlockSpec(memory_space=pltpu.VMEM)
    hbm = pl.BlockSpec(memory_space=pltpu.HBM)
    dma = pltpu.SemaphoreType.DMA
    scratch = (
        [pltpu.VMEM((2, half, 2 * tok, hd), BF) for _ in range(2)]
        + [
            pltpu.VMEM((2, half, 2, tok, hd), BF),
            pltpu.VMEM((9 * third, 2, tok, hd), BF),
            pltpu.VMEM((9 * third, 2, tok, hd), BF),
            pltpu.VMEM((2, 6, third, 2, tok, hd), BF),
            pltpu.VMEM((9, 16, hd), F32),
        ]
        + [pltpu.VMEM((tok, cols), BF) for _ in range(5)]
        + [pltpu.VMEM((tok, heads), F32), pltpu.SMEM((4, heads), jnp.int32), dma((7,))]
        + [
            pltpu.VMEM((heads * 4, tok, hd), BF),
            pltpu.VMEM((18, third, tok, hd), BF),
            pltpu.VMEM((9 * third, tok, hd), BF),
            pltpu.VMEM((9 * third, tok, hd), BF),
            pltpu.VMEM((heads, 2, 2 * tok, hd), F32),
            pltpu.VMEM((heads, tok, hd), F32),
            pltpu.VMEM((2, half, 2, tok, hd), BF),
            pltpu.VMEM((2, half, 2, tok, hd), BF),
            pltpu.SMEM((18 * third,), jnp.int32),
            pltpu.SMEM((18 * third,), jnp.int32),
            pltpu.SMEM((heads * 4,), jnp.int32),
            pltpu.SMEM((heads * 4,), jnp.int32),
        ]
    )
    for sem in ((2, 2, third), (2,), (2,), (2, 6, third), (6,), (2, 9, third), (2, third)):
        scratch += [dma(sem), dma(sem)]
    for _ in range(4):
        scratch += [pltpu.VMEM((half - third + 1 if k == 0 else 1, 2, tok, hd), BF) for k in range(third)]
    dq, dk, dv = pl.pallas_call(
        functools.partial(kernel, n_sh, n_sw, half, hd),
        out_shape=[pltpu.VMEM((tok, cols), BF)] * 3,
        in_specs=[hbm] * 7,
        out_specs=[vmem] * 3,
        scratch_shapes=scratch,
        compiler_params=pltpu.CompilerParams(
            collective_id=0, has_side_effects=True, vmem_limit_bytes=32 * 2**20
        ),
    )(flat(queries), flat(keys), flat(values), flat(attn_grad), flat(attn_out), flat(log_sum), place(window_dirs.T, pltpu.HBM))
    dq, dk, dv = pl.pallas_call(
        hand_out,
        out_shape=[jax.ShapeDtypeStruct((tok, cols), BF)] * 3,
        in_specs=[vmem] * 3,
        out_specs=[hbm] * 3,
        scratch_shapes=[dma((3,))],
    )(*(place(array, pltpu.VMEM) for array in (dq, dk, dv)))
    return tuple(array.reshape(shape) for array in (dq, dk, dv))


def solution(mesh):
    spec = P("tp", "sh", "sw", None)
    return jax.shard_map(
        functools.partial(local, mesh.shape["sh"], mesh.shape["sw"]),
        mesh=mesh,
        in_specs=(spec,) * 6 + (P(),),
        out_specs=(spec,) * 3,
        check_vma=False,
    )
```

```python
import functools

import jax
import jax.numpy as jnp
from jax import lax
from jax.experimental import pallas as pl
from jax.experimental.pallas import tpu as pltpu
from jax.sharding import PartitionSpec as P

E_OF = (1, 7, 4, 0, 3, 2, 8, 5)
BF = jnp.bfloat16
F32 = jnp.float32
NT = (((1,), (1,)), ((), ()))
TN = (((0,), (0,)), ((), ()))


SIDES = (0, 1, 2, 3, 4, 5, 7, 8)
ROW_STEP = (0, -1, 1)
COL_STEP = (-1, 1, 0)


def kernel(
    n_sh, n_sw, half, hd,
    q_in, k_in, v_in, g_in, o_in, lse_in, wd_in,
    dq_out, dk_out, dv_out,
    kvx, qg, zq, pieces0, pieces1, packed, stats,
    q_ref, k_ref, v_ref, g_ref, o_ref, lse_ref, wd_ref, in_sem,
    dqp, dqs, dqr0, dqr1, own_kv, own_q, xsend, xback,
    head_of, src_of, flat_of, e_of,
    zs, zr, zts, ztr, xs, xr, ws, wr, wts, wtr, bs, br, rxr, *zbs,
):
    row = lax.axis_index("sh")
    col = lax.axis_index("sw")
    part = lax.axis_index("tp")
    pieces = (pieces0, pieces1)
    dqr = (dqr0, dqr1)
    third = half // 2
    zb = [[zbs[(run * 2 + i) * third:(run * 2 + i + 1) * third] for i in (0, 1)] for run in (0, 1)]
    tok = q_ref.shape[0]
    arguments = (
        (q_in, q_ref), (g_in, g_ref), (k_in, k_ref), (v_in, v_ref), (wd_in, wd_ref), (o_in, o_ref), (lse_in, lse_ref),
    )
    loads = [pltpu.make_async_copy(src, dst, in_sem.at[i]) for i, (src, dst) in enumerate(arguments)]
    for load in loads:
        load.start()
    scale = hd ** -0.5
    row_ok = lambda step: (row + step >= 0) & (row + step < n_sh)
    col_ok = lambda step: (col + step >= 0) & (col + step < n_sw)
    spans = [(0, half - third + 1)] + [(half - third + k, half - third + k + 1) for k in range(1, third)]
    MESH = pl.DeviceIdType.MESH

    def sent_to(e):
        return row_ok(ROW_STEP[e % 3]) & col_ok(COL_STEP[e // 3])

    def came_from(e):
        return row_ok(-ROW_STEP[e % 3]) & col_ok(-COL_STEP[e // 3])

    def remote(src, dst, ssem, rsem, device):
        return pltpu.make_async_remote_copy(
            src_ref=src, dst_ref=dst, send_sem=ssem, recv_sem=rsem, device_id=device, device_id_type=MESH,
        )

    def copy_z(run, i, k, a):
        lo, hi = ((run * half + h) * hd for h in spans[k])
        src = (q_in, g_in)[a].at[:, lo:hi]
        return remote(src, zb[run][i][k].at[a], zs.at[i], zr.at[run, i, k], {"sh": row + 2 * i - 1})

    def copy_zstat(i):
        return remote(stats.at[6], stats.at[7 + i], zts.at[i], ztr.at[i], {"sh": row + 2 * i - 1})

    def copy_x(run, a):
        cols = slice(run * half * hd, (run + 1) * half * hd)
        return remote((k_in, v_in)[a].at[:, cols], kvx.at[a, :, cols], xs.at[0], xr.at[run], {"tp": 1 - part})

    def copy_w(run, e, k):
        span = pl.ds(k, 1) if e % 3 else pl.ds(0, third)
        at = pl.ds(e * third + k, 1) if e % 3 else pl.ds(e * third, third)
        return remote(
            packed.at[run, e, span], pieces[run].at[at], ws.at[e // 3], wr.at[run, e // 3], {"sw": col + COL_STEP[e // 3]},
        )

    def copy_wstat(e):
        return remote(stats.at[6 + e % 3], stats.at[e], wts.at[e // 3], wtr.at[e // 3], {"sw": col + COL_STEP[e // 3]})

    def copy_back(run, e, k):
        at = run * 9 + e
        home = {"sh": row - ROW_STEP[e % 3], "sw": col - COL_STEP[e // 3]}
        return remote(dqs.at[at, k], dqr[run].at[e * third + k], bs.at[e % 3], br.at[run, e % 3], home)

    def copy_xback(run, h):
        return remote(xsend.at[run, h], xback.at[run, h], xs.at[0], rxr.at[run], {"tp": 1 - part})

    n_rows = row_ok(-1).astype(jnp.int32) + row_ok(1).astype(jnp.int32)
    n_cols = col_ok(-1).astype(jnp.int32) + col_ok(1).astype(jnp.int32)

    def drain(ref, sem):
        pltpu.make_async_copy(ref, ref, sem).wait()

    barrier = pltpu.get_barrier_semaphore()
    pl.semaphore_signal(barrier, inc=1, device_id={"tp": 1 - part}, device_id_type=MESH)
    count = 1
    for e in SIDES:
        @pl.when(sent_to(e))
        def _():
            near = {"sh": row + ROW_STEP[e % 3], "sw": col + COL_STEP[e // 3]}
            pl.semaphore_signal(barrier, inc=1, device_id=near, device_id_type=MESH)
        count = count + sent_to(e).astype(jnp.int32)

    pl.semaphore_wait(barrier, count)

    def send_z(run):
        for k in range(third):
            for i in (0, 1):
                @pl.when(row_ok(2 * i - 1))
                def _():
                    copy_z(run, i, k, 0).start()
                    copy_z(run, i, k, 1).start()

    send_z(0)
    for run in (0, 1):
        for a in (0, 1):
            copy_x(run, a).start()

    for i in (4, 0, 1, 5, 6):
        loads[i].wait()
    for run in (0, 1):
        seen = jnp.int32(0)
        heads = [jnp.int32(0) for _ in range(third)]
        slots = [jnp.int32(0) for _ in range(third)]
        for h in range(half):
            dirs = [wd_ref[j, run * half + h] for j in range(4)]
            bits = [(d & 1, (d >> 1) & 1, d >> 2) for d in dirs]
            one = [(1 + 15 * a) * (1 + 255 * b) * (1 + 65535 * c) for a, b, c in bits]
            for j in range(4):
                field = seen & (one[j] * 15)
                here = [field == one[j] * s for s in range(third)]
                rank = sum(here[s].astype(jnp.int32) * s for s in range(1, third))
                n = dirs[j] + bits[j][2]
                up = (n * 11) >> 5
                over = n - 3 * up
                e = jnp.where(over == 1, 6, jnp.where(over == 2, 3, 0)) + jnp.where(up == 1, 0, jnp.where(up == 2, 2, 1))
                flat_of[(run * half + h) * 4 + j] = e * third + rank
                e_of[(run * half + h) * 4 + j] = e
                for s in range(third):
                    mine = jnp.where(here[s], one[j], 0)
                    if h:
                        heads[s] = heads[s] + mine * h
                    if j:
                        slots[s] = slots[s] + mine * j
            seen = seen + (one[0] + one[1]) + (one[2] + one[3])
        for d in range(8):
            for s in range(third):
                h = jnp.minimum(lax.shift_right_logical(heads[s], 4 * d) & 15, half - 1)
                head_of[(run * 9 + E_OF[d]) * third + s] = h
                src_of[(run * 9 + E_OF[d]) * third + s] = (run * half + h) * 4 + jnp.minimum(lax.shift_right_logical(slots[s], 4 * d) & 15, 3)

    lane = lax.broadcasted_iota(jnp.int32, (tok, hd), 1)
    table = jnp.zeros((tok, hd), F32)
    for at in range(2 * half):
        cols = slice(at * hd, (at + 1) * hd)
        delta = jnp.sum(g_ref[:, cols].astype(F32) * o_ref[:, cols].astype(F32), axis=1, keepdims=True)
        table = jnp.where(lane == at, lse_ref[:, at:at + 1], table)
        table = jnp.where(lane == 16 + at, delta, table)
    turned = jnp.concatenate([table, jnp.zeros((hd - tok, hd), F32)], axis=0).T
    stats[6] = turned[:16] + pltpu.roll(turned[16:32], tok, 1)
    for i in (0, 1):
        @pl.when(row_ok(2 * i - 1))
        def _():
            copy_zstat(i).start()
    send_z(1)

    def pack(run, e, s):
        i = e % 3
        h = head_of[(run * 9 + e) * third + s]
        block = zq[run * 2 + i - 1, h] if i else qg[run, h]
        if e // 3 == 2:
            pieces[run][e * third + s] = block
        else:
            packed[run, e, s] = block

    for run in (0, 1):
        for h in range(half):
            cols = slice((run * half + h) * hd, (run * half + h + 1) * hd)
            qg[run, h, 0] = q_ref[:, cols]
            qg[run, h, 1] = g_ref[:, cols]
    for run in (0, 1):
        for e in (0, 3):
            @pl.when(sent_to(e))
            def _():
                for s in range(third):
                    pack(run, e, s)
                copy_w(run, e, 0).start()
    for e in (0, 3):
        @pl.when(sent_to(e))
        def _():
            copy_wstat(e).start()

    for e in SIDES:
        @pl.when(jnp.logical_not(came_from(e)))
        def _():
            stats[e] = jnp.zeros(stats.shape[1:], F32)
            for run in (0, 1):
                pieces[run][e * third:(e + 1) * third] = jnp.zeros((third,) + pieces0.shape[1:], BF)

        @pl.when(jnp.logical_not(sent_to(e)))
        def _():
            for run in (0, 1):
                dqr[run][e * third:(e + 1) * third] = jnp.zeros((third,) + dqr0.shape[1:], BF)

    def relay(run, k):
        for i in (1, 2):
            @pl.when(row_ok(-ROW_STEP[i]))
            def _():
                held = zb[run][i - 1][k]
                drain(held, zr.at[run, i - 1, k])
                for n, h in enumerate(range(*spans[k])):
                    for a in (0, 1):
                        zq[run * 2 + i - 1, h, a] = held[a, :, n * hd:(n + 1) * hd]
                if run == 0 and k == third - 1:
                    copy_zstat(i - 1).wait_recv()
                for e in (i, 3 + i):
                    @pl.when(col_ok(COL_STEP[e // 3]))
                    def _():
                        pack(run, e, k)
                        copy_w(run, e, k).start()
                        if run == 0 and k == third - 1:
                            copy_wstat(e).start()
                pack(run, 6 + i, k)

    def products(keys, vals, q, g, lse, delta):
        scores = lax.dot_general(keys, q, NT, preferred_element_type=F32)
        prob = jnp.exp(scores * scale - lse)
        grad_prob = lax.dot_general(vals, g, NT, preferred_element_type=F32)
        score_bf = (prob * (grad_prob - delta)).astype(BF)
        dv = jnp.dot(prob.astype(BF), g, preferred_element_type=F32)
        dk = jnp.dot(score_bf, q, preferred_element_type=F32) * scale
        dq = lax.dot_general(score_bf, keys, TN, preferred_element_type=F32) * scale
        return dq, dk, dv

    def keys_of(at):
        cols = slice(at * hd, (at + 1) * hd)
        return (jnp.concatenate([mine[:, cols], other[:, cols]], axis=0) for mine, other in ((k_ref, kvx.at[0]), (v_ref, kvx.at[1])))

    def own(run):
        for h in range(half):
            at = run * half + h
            cols = slice(at * hd, (at + 1) * hd)
            stat = stats[6, at:at + 1, :]
            dq, dk, dv = products(
                *keys_of(at), q_ref[:, cols], g_ref[:, cols], stat[:, :tok], pltpu.roll(stat, tok, 1)[:, :tok],
            )
            own_q[at] = dq
            own_kv[at, 0] = dk
            own_kv[at, 1] = dv

    first = lax.broadcasted_iota(jnp.int32, (1, hd), 1) < tok

    def near(run, h):
        at = run * half + h
        where = [flat_of[at * 4 + j] for j in range(4)]
        q = jnp.concatenate([pieces[run][w, 0] for w in where], axis=0)
        g = jnp.concatenate([pieces[run][w, 1] for w in where], axis=0)
        stat = [stats[e_of[at * 4 + j], at:at + 1, :] for j in range(4)]
        turn = [pltpu.roll(s, tok, 1) for s in stat]
        lse = jnp.concatenate([jnp.where(first, stat[j], turn[j + 1]) for j in (0, 2)], axis=1)
        delta = jnp.concatenate([jnp.where(first, turn[j], stat[j + 1]) for j in (0, 2)], axis=1)
        dq, dk, dv = products(*keys_of(at), q, g, lse, delta)
        for j in range(4):
            dqp[at * 4 + j] = dq[j * tok:(j + 1) * tok].astype(BF)
        for a, grad in ((0, dk), (1, dv)):
            total = own_kv[at, a] + grad
            own_kv[at, a, :tok] = total[:tok]
            xsend[run, h, a] = total[tok:].astype(BF)

    def arrived(run):
        for c in (0, 1):
            for v in (0, 1, 2):
                @pl.when(col_ok(-COL_STEP[c]) & (n_rows == v))
                def _():
                    drain(pieces[run].at[0:third * (1 + v)], wr.at[run, c])
                    if run == 0:
                        drain(stats.at[0:1 + v], wtr.at[c])

    def batch(run, k):
        for h in range(*spans[k]):
            near(run, h)
            copy_xback(run, h).start()
        for e in SIDES:
            dqs[run * 9 + e, k] = dqp[src_of[(run * 9 + e) * third + k]]

            @pl.when(came_from(e))
            def _():
                copy_back(run, e, k).start()

    def finish_kv(run):
        drain(xback.at[run], rxr.at[run])
        for h in range(half):
            cols = slice((run * half + h) * hd, (run * half + h + 1) * hd)
            for a, out in ((0, dk_out), (1, dv_out)):
                out[:, cols] = (own_kv[run * half + h, a, :tok] + xback[run, h, a].astype(F32)).astype(BF)

    def finish_q(run):
        for i in range(3):
            for v in (0, 1, 2):
                if v or i:
                    @pl.when(row_ok(ROW_STEP[i]) & (n_cols == v))
                    def _():
                        drain(dqr[run].at[0:third * (v + (i > 0))], br.at[run, i])
        for h in range(half):
            at = run * half + h
            total = own_q[at]
            for j in range(4):
                total = total + dqr[run][flat_of[at * 4 + j]].astype(F32)
            dq_out[:, at * hd:(at + 1) * hd] = total.astype(BF)

    def got_x(run):
        drain(kvx.at[:, :, run * half * hd:(run + 1) * half * hd], xr.at[run])

    loads[2].wait()
    loads[3].wait()
    for k in range(third):
        relay(0, k)
    got_x(0)
    own(0)
    relay(1, 0)
    arrived(0)
    for k in range(third):
        batch(0, k)
    for k in range(1, third):
        relay(1, k)
    got_x(1)
    own(1)
    arrived(1)
    for k in range(third):
        batch(1, k)
    finish_kv(0)
    finish_q(0)
    finish_kv(1)
    finish_q(1)

    drain(dqp, xs.at[0])
    for i in (0, 1):
        @pl.when(row_ok(2 * i - 1))
        def _():
            drain(dqp.at[0:4 * half], zs.at[i])
            copy_zstat(i).wait_send()
    for v in (0, 1, 2):
        for c in (0, 1):
            @pl.when(col_ok(COL_STEP[c]) & (n_rows == v))
            def _():
                drain(dqp.at[0:4 * third * (1 + v)], ws.at[c])
                drain(stats.at[0:1 + v], wts.at[c])
        for i in range(3):
            if v or i:
                @pl.when(row_ok(-ROW_STEP[i]) & (n_cols == v))
                def _():
                    drain(dqp.at[0:2 * third * (v + (i > 0))], bs.at[i])


def hand_out(a_in, b_in, c_in, a_out, b_out, c_out, out_sem):
    outs = [
        pltpu.make_async_copy(src, dst, out_sem.at[i])
        for i, (src, dst) in enumerate(((a_in, a_out), (b_in, b_out), (c_in, c_out)))
    ]
    for copy in outs:
        copy.start()
    for copy in outs:
        copy.wait()


def local(n_sh, n_sw, queries, keys, values, attn_out, attn_grad, log_sum, window_dirs):
    shape = queries.shape
    tok = shape[0] * shape[1] * shape[2]
    cols = shape[3]
    heads = log_sum.shape[3]
    half = heads // 2
    third = half // 2
    hd = cols // heads
    place = pltpu.with_memory_space_constraint
    flat = lambda array: place(array.reshape(tok, array.shape[3]), pltpu.HBM)
    vmem = pl.BlockSpec(memory_space=pltpu.VMEM)
    hbm = pl.BlockSpec(memory_space=pltpu.HBM)
    dma = pltpu.SemaphoreType.DMA
    scratch = (
        [
            pltpu.VMEM((2, tok, cols), BF),
            pltpu.VMEM((2, half, 2, tok, hd), BF),
            pltpu.VMEM((4, half, 2, tok, hd), BF),
        ]
        + [
            pltpu.VMEM((9 * third, 2, tok, hd), BF),
            pltpu.VMEM((9 * third, 2, tok, hd), BF),
            pltpu.VMEM((2, 6, third, 2, tok, hd), BF),
            pltpu.VMEM((9, 16, hd), F32),
        ]
        + [pltpu.VMEM((tok, cols), BF) for _ in range(5)]
        + [pltpu.VMEM((tok, heads), F32), pltpu.SMEM((4, heads), jnp.int32), dma((7,))]
        + [
            pltpu.VMEM((heads * 4, tok, hd), BF),
            pltpu.VMEM((18, third, tok, hd), BF),
            pltpu.VMEM((9 * third, tok, hd), BF),
            pltpu.VMEM((9 * third, tok, hd), BF),
            pltpu.VMEM((heads, 2, 2 * tok, hd), F32),
            pltpu.VMEM((heads, tok, hd), F32),
            pltpu.VMEM((2, half, 2, tok, hd), BF),
            pltpu.VMEM((2, half, 2, tok, hd), BF),
            pltpu.SMEM((18 * third,), jnp.int32),
            pltpu.SMEM((18 * third,), jnp.int32),
            pltpu.SMEM((heads * 4,), jnp.int32),
            pltpu.SMEM((heads * 4,), jnp.int32),
        ]
    )
    sems = ((2,), (2, 2, third), (2,), (2,), (1,), (2,), (2,), (2, 2), (2,), (2,), (3,), (2, 3), (2,))
    scratch += [dma(sem) for sem in sems]
    for _ in range(4):
        scratch += [pltpu.VMEM((2, tok, (half - third + 1 if k == 0 else 1) * hd), BF) for k in range(third)]
    dq, dk, dv = pl.pallas_call(
        functools.partial(kernel, n_sh, n_sw, half, hd),
        out_shape=[pltpu.VMEM((tok, cols), BF)] * 3,
        in_specs=[hbm] * 7,
        out_specs=[vmem] * 3,
        scratch_shapes=scratch,
        compiler_params=pltpu.CompilerParams(
            collective_id=0, has_side_effects=True, vmem_limit_bytes=32 * 2**20
        ),
    )(flat(queries), flat(keys), flat(values), flat(attn_grad), flat(attn_out), flat(log_sum), place(window_dirs.T, pltpu.HBM))
    dq, dk, dv = pl.pallas_call(
        hand_out,
        out_shape=[jax.ShapeDtypeStruct((tok, cols), BF)] * 3,
        in_specs=[vmem] * 3,
        out_specs=[hbm] * 3,
        scratch_shapes=[dma((3,))],
    )(*(place(array, pltpu.VMEM) for array in (dq, dk, dv)))
    return tuple(array.reshape(shape) for array in (dq, dk, dv))


def solution(mesh):
    spec = P("tp", "sh", "sw", None)
    return jax.shard_map(
        functools.partial(local, mesh.shape["sh"], mesh.shape["sw"]),
        mesh=mesh,
        in_specs=(spec,) * 6 + (P(),),
        out_specs=(spec,) * 3,
        check_vma=False,
    )
```

```python
import functools

import jax
import jax.numpy as jnp
from jax import lax
from jax.experimental import pallas as pl
from jax.experimental.pallas import tpu as pltpu
from jax.sharding import PartitionSpec as P

E_OF = (1, 7, 4, 0, 3, 2, 8, 5)
BF = jnp.bfloat16
F32 = jnp.float32
NT = (((1,), (1,)), ((), ()))
TN = (((0,), (0,)), ((), ()))


SIDES = (0, 1, 2, 3, 4, 5, 7, 8)
ROW_STEP = (0, -1, 1)
COL_STEP = (-1, 1, 0)


def kernel(
    n_sh, n_sw, half, hd,
    q_in, k_in, v_in, g_in, o_in, lse_in, wd_in,
    dq_out, dk_out, dv_out,
    kvx, qg, zq, pieces0, pieces1, packed, stats,
    q_ref, k_ref, v_ref, g_ref, o_ref, lse_ref, wd_ref, in_sem,
    dqp, dqs, dqr0, dqr1, own_kv, own_q, xsend, xback,
    head_of, src_of, flat_of, e_of,
    zs, zr, zts, ztr, xs, xr, ws, wr, wts, wtr, bs, br, rxr, *zbs,
):
    row = lax.axis_index("sh")
    col = lax.axis_index("sw")
    part = lax.axis_index("tp")
    pieces = (pieces0, pieces1)
    dqr = (dqr0, dqr1)
    third = half // 2
    zb = [[zbs[(run * 2 + i) * third:(run * 2 + i + 1) * third] for i in (0, 1)] for run in (0, 1)]
    tok = q_ref.shape[0]
    arguments = (
        (q_in, q_ref), (g_in, g_ref), (k_in, k_ref), (v_in, v_ref), (wd_in, wd_ref), (o_in, o_ref), (lse_in, lse_ref),
    )
    loads = [pltpu.make_async_copy(src, dst, in_sem.at[i]) for i, (src, dst) in enumerate(arguments)]
    for load in loads:
        load.start()
    scale = hd ** -0.5
    row_ok = lambda step: (row + step >= 0) & (row + step < n_sh)
    col_ok = lambda step: (col + step >= 0) & (col + step < n_sw)
    spans = [(0, half - third + 1)] + [(half - third + k, half - third + k + 1) for k in range(1, third)]
    MESH = pl.DeviceIdType.MESH

    def sent_to(e):
        return row_ok(ROW_STEP[e % 3]) & col_ok(COL_STEP[e // 3])

    def came_from(e):
        return row_ok(-ROW_STEP[e % 3]) & col_ok(-COL_STEP[e // 3])

    def remote(src, dst, ssem, rsem, device):
        return pltpu.make_async_remote_copy(
            src_ref=src, dst_ref=dst, send_sem=ssem, recv_sem=rsem, device_id=device, device_id_type=MESH,
        )

    def copy_z(run, i, k, a):
        lo, hi = ((run * half + h) * hd for h in spans[k])
        src = (q_in, g_in)[a].at[:, lo:hi]
        return remote(src, zb[run][i][k].at[a], zs.at[i], zr.at[run, i, k], {"sh": row + 2 * i - 1})

    def copy_zstat(i):
        return remote(stats.at[6], stats.at[7 + i], zts.at[i], ztr.at[i], {"sh": row + 2 * i - 1})

    def copy_x(run, a):
        cols = slice(run * half * hd, (run + 1) * half * hd)
        return remote((k_in, v_in)[a].at[:, cols], kvx.at[a, :, cols], xs.at[0], xr.at[run], {"tp": 1 - part})

    def copy_w(run, e, k):
        span = pl.ds(k, 1) if e % 3 else pl.ds(0, third)
        at = pl.ds(e * third + k, 1) if e % 3 else pl.ds(e * third, third)
        return remote(
            packed.at[run, e, span], pieces[run].at[at], ws.at[e // 3], wr.at[run, e // 3], {"sw": col + COL_STEP[e // 3]},
        )

    def copy_wstat(e):
        return remote(stats.at[6 + e % 3], stats.at[e], wts.at[e // 3], wtr.at[e // 3], {"sw": col + COL_STEP[e // 3]})

    def copy_back(run, e, k):
        at = run * 9 + e
        home = {"sh": row - ROW_STEP[e % 3], "sw": col - COL_STEP[e // 3]}
        return remote(dqs.at[at, k], dqr[run].at[e * third + k], bs.at[e % 3], br.at[run, e % 3], home)

    def copy_xback(run, h):
        return remote(xsend.at[run, h], xback.at[run, h], xs.at[0], rxr.at[run], {"tp": 1 - part})

    n_rows = row_ok(-1).astype(jnp.int32) + row_ok(1).astype(jnp.int32)
    n_cols = col_ok(-1).astype(jnp.int32) + col_ok(1).astype(jnp.int32)

    def drain(ref, sem):
        pltpu.make_async_copy(ref, ref, sem).wait()

    barrier = pltpu.get_barrier_semaphore()
    pl.semaphore_signal(barrier, inc=1, device_id={"tp": 1 - part}, device_id_type=MESH)
    count = 1
    for e in SIDES:
        @pl.when(sent_to(e))
        def _():
            near = {"sh": row + ROW_STEP[e % 3], "sw": col + COL_STEP[e // 3]}
            pl.semaphore_signal(barrier, inc=1, device_id=near, device_id_type=MESH)
        count = count + sent_to(e).astype(jnp.int32)

    pl.semaphore_wait(barrier, count)

    def send_z(run):
        for k in range(third):
            for i in (0, 1):
                @pl.when(row_ok(2 * i - 1))
                def _():
                    copy_z(run, i, k, 0).start()
                    copy_z(run, i, k, 1).start()

    send_z(0)
    for run in (0, 1):
        for a in (0, 1):
            copy_x(run, a).start()

    for i in (4, 0, 1, 5, 6):
        loads[i].wait()
    for run in (0, 1):
        seen = jnp.int32(0)
        heads = [jnp.int32(0) for _ in range(third)]
        slots = [jnp.int32(0) for _ in range(third)]
        for h in range(half):
            dirs = [wd_ref[j, run * half + h] for j in range(4)]
            bits = [(d & 1, (d >> 1) & 1, d >> 2) for d in dirs]
            one = [(1 + 15 * a) * (1 + 255 * b) * (1 + 65535 * c) for a, b, c in bits]
            for j in range(4):
                field = seen & (one[j] * 15)
                here = [field == one[j] * s for s in range(third)]
                rank = sum(here[s].astype(jnp.int32) * s for s in range(1, third))
                n = dirs[j] + bits[j][2]
                up = (n * 11) >> 5
                over = n - 3 * up
                e = jnp.where(over == 1, 6, jnp.where(over == 2, 3, 0)) + jnp.where(up == 1, 0, jnp.where(up == 2, 2, 1))
                flat_of[(run * half + h) * 4 + j] = e * third + rank
                e_of[(run * half + h) * 4 + j] = e
                for s in range(third):
                    mine = jnp.where(here[s], one[j], 0)
                    if h:
                        heads[s] = heads[s] + mine * h
                    if j:
                        slots[s] = slots[s] + mine * j
            seen = seen + (one[0] + one[1]) + (one[2] + one[3])
        for d in range(8):
            for s in range(third):
                h = jnp.minimum(lax.shift_right_logical(heads[s], 4 * d) & 15, half - 1)
                head_of[(run * 9 + E_OF[d]) * third + s] = h
                src_of[(run * 9 + E_OF[d]) * third + s] = (run * half + h) * 4 + jnp.minimum(lax.shift_right_logical(slots[s], 4 * d) & 15, 3)

    lane = lax.broadcasted_iota(jnp.int32, (tok, hd), 1)
    table = jnp.zeros((tok, hd), F32)
    for at in range(2 * half):
        cols = slice(at * hd, (at + 1) * hd)
        delta = jnp.sum(g_ref[:, cols].astype(F32) * o_ref[:, cols].astype(F32), axis=1, keepdims=True)
        table = jnp.where(lane == at, lse_ref[:, at:at + 1], table)
        table = jnp.where(lane == 16 + at, delta, table)
    turned = jnp.concatenate([table, jnp.zeros((hd - tok, hd), F32)], axis=0).T
    stats[6] = turned[:16] + pltpu.roll(turned[16:32], tok, 1)
    for i in (0, 1):
        @pl.when(row_ok(2 * i - 1))
        def _():
            copy_zstat(i).start()
    send_z(1)

    def pack(run, e, s):
        i = e % 3
        h = head_of[(run * 9 + e) * third + s]
        block = zq[run * 2 + i - 1, h] if i else qg[run, h]
        if e // 3 == 2:
            pieces[run][e * third + s] = block
        else:
            packed[run, e, s] = block

    for run in (0, 1):
        for h in range(half):
            cols = slice((run * half + h) * hd, (run * half + h + 1) * hd)
            qg[run, h, 0] = q_ref[:, cols]
            qg[run, h, 1] = g_ref[:, cols]
    for run in (0, 1):
        for e in (0, 3):
            @pl.when(sent_to(e))
            def _():
                for s in range(third):
                    pack(run, e, s)
                copy_w(run, e, 0).start()
    for e in (0, 3):
        @pl.when(sent_to(e))
        def _():
            copy_wstat(e).start()

    for e in SIDES:
        @pl.when(jnp.logical_not(came_from(e)))
        def _():
            stats[e] = jnp.zeros(stats.shape[1:], F32)
            for run in (0, 1):
                pieces[run][e * third:(e + 1) * third] = jnp.zeros((third,) + pieces0.shape[1:], BF)

        @pl.when(jnp.logical_not(sent_to(e)))
        def _():
            for run in (0, 1):
                dqr[run][e * third:(e + 1) * third] = jnp.zeros((third,) + dqr0.shape[1:], BF)

    def relay(run, k):
        for i in (1, 2):
            @pl.when(row_ok(-ROW_STEP[i]))
            def _():
                held = zb[run][i - 1][k]
                drain(held, zr.at[run, i - 1, k])
                for n, h in enumerate(range(*spans[k])):
                    for a in (0, 1):
                        zq[run * 2 + i - 1, h, a] = held[a, :, n * hd:(n + 1) * hd]
                if run == 0 and k == third - 1:
                    copy_zstat(i - 1).wait_recv()
                for e in (i, 3 + i):
                    @pl.when(col_ok(COL_STEP[e // 3]))
                    def _():
                        pack(run, e, k)
                        copy_w(run, e, k).start()
                        if run == 0 and k == third - 1:
                            copy_wstat(e).start()
                pack(run, 6 + i, k)

    def products(keys, vals, q, g, lse, delta):
        scores = lax.dot_general(keys, q, NT, preferred_element_type=F32)
        prob = jnp.exp(scores * scale - lse)
        grad_prob = lax.dot_general(vals, g, NT, preferred_element_type=F32)
        score_bf = (prob * (grad_prob - delta)).astype(BF)
        dv = jnp.dot(prob.astype(BF), g, preferred_element_type=F32)
        dk = jnp.dot(score_bf, q, preferred_element_type=F32) * scale
        dq = lax.dot_general(score_bf, keys, TN, preferred_element_type=F32) * scale
        return dq, dk, dv

    def keys_of(at):
        cols = slice(at * hd, (at + 1) * hd)
        return (jnp.concatenate([mine[:, cols], other[:, cols]], axis=0) for mine, other in ((k_ref, kvx.at[0]), (v_ref, kvx.at[1])))

    def own(run):
        for h in range(half):
            at = run * half + h
            cols = slice(at * hd, (at + 1) * hd)
            stat = stats[6, at:at + 1, :]
            dq, dk, dv = products(
                *keys_of(at), q_ref[:, cols], g_ref[:, cols], stat[:, :tok], pltpu.roll(stat, tok, 1)[:, :tok],
            )
            own_q[at] = dq
            own_kv[at, 0] = dk
            own_kv[at, 1] = dv

    first = lax.broadcasted_iota(jnp.int32, (1, hd), 1) < tok

    def near(run, h):
        at = run * half + h
        where = [flat_of[at * 4 + j] for j in range(4)]
        q = jnp.concatenate([pieces[run][w, 0] for w in where], axis=0)
        g = jnp.concatenate([pieces[run][w, 1] for w in where], axis=0)
        stat = [stats[e_of[at * 4 + j], at:at + 1, :] for j in range(4)]
        turn = [pltpu.roll(s, tok, 1) for s in stat]
        lse = jnp.concatenate([jnp.where(first, stat[j], turn[j + 1]) for j in (0, 2)], axis=1)
        delta = jnp.concatenate([jnp.where(first, turn[j], stat[j + 1]) for j in (0, 2)], axis=1)
        dq, dk, dv = products(*keys_of(at), q, g, lse, delta)
        for j in range(4):
            dqp[at * 4 + j] = dq[j * tok:(j + 1) * tok].astype(BF)
        for a, grad in ((0, dk), (1, dv)):
            total = own_kv[at, a] + grad
            own_kv[at, a, :tok] = total[:tok]
            xsend[run, h, a] = total[tok:].astype(BF)

    def arrived(run):
        for c in (0, 1):
            for v in (0, 1, 2):
                @pl.when(col_ok(-COL_STEP[c]) & (n_rows == v))
                def _():
                    drain(pieces[run].at[0:third * (1 + v)], wr.at[run, c])
                    if run == 0:
                        drain(stats.at[0:1 + v], wtr.at[c])

    def nears(run, *heads):
        for h in heads:
            near(run, h)
        for h in heads:
            copy_xback(run, h).start()

    def back(run, k):
        for e in SIDES:
            dqs[run * 9 + e, k] = dqp[src_of[(run * 9 + e) * third + k]]
        for e in SIDES:
            @pl.when(came_from(e))
            def _():
                copy_back(run, e, k).start()

    def finish_kv(run):
        drain(xback.at[run], rxr.at[run])
        for h in range(half):
            cols = slice((run * half + h) * hd, (run * half + h + 1) * hd)
            for a, out in ((0, dk_out), (1, dv_out)):
                out[:, cols] = (own_kv[run * half + h, a, :tok] + xback[run, h, a].astype(F32)).astype(BF)

    def finish_q(run):
        for i in range(3):
            for v in (0, 1, 2):
                if v or i:
                    @pl.when(row_ok(ROW_STEP[i]) & (n_cols == v))
                    def _():
                        drain(dqr[run].at[0:third * (v + (i > 0))], br.at[run, i])
        for h in range(half):
            at = run * half + h
            total = own_q[at]
            for j in range(4):
                total = total + dqr[run][flat_of[at * 4 + j]].astype(F32)
            dq_out[:, at * hd:(at + 1) * hd] = total.astype(BF)

    def got_x(run):
        drain(kvx.at[:, :, run * half * hd:(run + 1) * half * hd], xr.at[run])

    loads[2].wait()
    loads[3].wait()
    relay(0, 0)
    relay(0, 1)
    relay(0, 2)
    got_x(0)
    own(0)
    relay(1, 0)
    arrived(0)
    nears(0,0,1)
    relay(1,1)
    nears(0,2,3)
    relay(1,2)
    nears(0,4,5)
    back(0, 0)
    back(0, 1)
    back(0, 2)
    got_x(1)
    own(1)
    arrived(1)
    nears(1, 0, 1)
    nears(1, 2, 3)
    back(1, 0)
    nears(1, 4, 5)
    back(1, 1)
    back(1, 2)
    finish_kv(0)
    finish_q(0)
    finish_kv(1)
    finish_q(1)

    drain(dqp, xs.at[0])
    for i in (0, 1):
        @pl.when(row_ok(2 * i - 1))
        def _():
            drain(dqp.at[0:4 * half], zs.at[i])
            copy_zstat(i).wait_send()
    for v in (0, 1, 2):
        for c in (0, 1):
            @pl.when(col_ok(COL_STEP[c]) & (n_rows == v))
            def _():
                drain(dqp.at[0:4 * third * (1 + v)], ws.at[c])
                drain(stats.at[0:1 + v], wts.at[c])
        for i in range(3):
            if v or i:
                @pl.when(row_ok(-ROW_STEP[i]) & (n_cols == v))
                def _():
                    drain(dqp.at[0:2 * third * (v + (i > 0))], bs.at[i])


def hand_out(a_in, b_in, c_in, a_out, b_out, c_out, out_sem):
    outs = [
        pltpu.make_async_copy(src, dst, out_sem.at[i])
        for i, (src, dst) in enumerate(((a_in, a_out), (b_in, b_out), (c_in, c_out)))
    ]
    for copy in outs:
        copy.start()
    for copy in outs:
        copy.wait()


def local(n_sh, n_sw, queries, keys, values, attn_out, attn_grad, log_sum, window_dirs):
    shape = queries.shape
    tok = shape[0] * shape[1] * shape[2]
    cols = shape[3]
    heads = log_sum.shape[3]
    half = heads // 2
    third = half // 2
    hd = cols // heads
    place = pltpu.with_memory_space_constraint
    flat = lambda array: place(array.reshape(tok, array.shape[3]), pltpu.HBM)
    vmem = pl.BlockSpec(memory_space=pltpu.VMEM)
    hbm = pl.BlockSpec(memory_space=pltpu.HBM)
    dma = pltpu.SemaphoreType.DMA
    scratch = (
        [
            pltpu.VMEM((2, tok, cols), BF),
            pltpu.VMEM((2, half, 2, tok, hd), BF),
            pltpu.VMEM((4, half, 2, tok, hd), BF),
        ]
        + [
            pltpu.VMEM((9 * third, 2, tok, hd), BF),
            pltpu.VMEM((9 * third, 2, tok, hd), BF),
            pltpu.VMEM((2, 6, third, 2, tok, hd), BF),
            pltpu.VMEM((9, 16, hd), F32),
        ]
        + [pltpu.VMEM((tok, cols), BF) for _ in range(5)]
        + [pltpu.VMEM((tok, heads), F32), pltpu.SMEM((4, heads), jnp.int32), dma((7,))]
        + [
            pltpu.VMEM((heads * 4, tok, hd), BF),
            pltpu.VMEM((18, third, tok, hd), BF),
            pltpu.VMEM((9 * third, tok, hd), BF),
            pltpu.VMEM((9 * third, tok, hd), BF),
            pltpu.VMEM((heads, 2, 2 * tok, hd), F32),
            pltpu.VMEM((heads, tok, hd), F32),
            pltpu.VMEM((2, half, 2, tok, hd), BF),
            pltpu.VMEM((2, half, 2, tok, hd), BF),
            pltpu.SMEM((18 * third,), jnp.int32),
            pltpu.SMEM((18 * third,), jnp.int32),
            pltpu.SMEM((heads * 4,), jnp.int32),
            pltpu.SMEM((heads * 4,), jnp.int32),
        ]
    )
    sems = ((2,), (2, 2, third), (2,), (2,), (1,), (2,), (2,), (2, 2), (2,), (2,), (3,), (2, 3), (2,))
    scratch += [dma(sem) for sem in sems]
    for _ in range(4):
        scratch += [pltpu.VMEM((2, tok, (half - third + 1 if k == 0 else 1) * hd), BF) for k in range(third)]
    dq, dk, dv = pl.pallas_call(
        functools.partial(kernel, n_sh, n_sw, half, hd),
        out_shape=[pltpu.VMEM((tok, cols), BF)] * 3,
        in_specs=[hbm] * 7,
        out_specs=[vmem] * 3,
        scratch_shapes=scratch,
        compiler_params=pltpu.CompilerParams(
            collective_id=0, has_side_effects=True, vmem_limit_bytes=32 * 2**20
        ),
    )(flat(queries), flat(keys), flat(values), flat(attn_grad), flat(attn_out), flat(log_sum), place(window_dirs.T, pltpu.HBM))
    dq, dk, dv = pl.pallas_call(
        hand_out,
        out_shape=[jax.ShapeDtypeStruct((tok, cols), BF)] * 3,
        in_specs=[vmem] * 3,
        out_specs=[hbm] * 3,
        scratch_shapes=[dma((3,))],
    )(*(place(array, pltpu.VMEM) for array in (dq, dk, dv)))
    return tuple(array.reshape(shape) for array in (dq, dk, dv))


def solution(mesh):
    spec = P("tp", "sh", "sw", None)
    return jax.shard_map(
        functools.partial(local, mesh.shape["sh"], mesh.shape["sw"]),
        mesh=mesh,
        in_specs=(spec,) * 6 + (P(),),
        out_specs=(spec,) * 3,
        check_vma=False,
    )
```

```python
import functools

import jax
import jax.numpy as jnp
from jax import lax
from jax.experimental import pallas as pl
from jax.experimental.pallas import tpu as pltpu
from jax.sharding import PartitionSpec as P

E_OF = (1, 7, 4, 0, 3, 2, 8, 5)
BF = jnp.bfloat16
F32 = jnp.float32
NT = (((1,), (1,)), ((), ()))
TN = (((0,), (0,)), ((), ()))


SIDES = (0, 1, 2, 3, 4, 5, 7, 8)
ROW_STEP = (0, -1, 1)
COL_STEP = (-1, 1, 0)


def kernel(
    n_sh, n_sw, half, hd,
    q_in, k_in, v_in, g_in, o_in, lse_in, wd_in,
    dq_out, dk_out, dv_out,
    kvx, qg, zq, packed, stats,
    q_ref, k_ref, v_ref, g_ref, o_ref, lse_ref, wd_ref, in_sem,
    dqp, dqs, dqr0, dqr1, own_kv, own_q, xsend, xback,
    head_of, src_of, flat_of, e_of, rank_of,
    zs, zr, zts, ztr, xs, xr, ws, wr, wts, wtr, bs, br, rxr, *zbs,
):
    row = lax.axis_index("sh")
    col = lax.axis_index("sw")
    part = lax.axis_index("tp")
    dqr = (dqr0, dqr1)
    third = half // 2
    pieces = (zbs[4 * third:5 * third], zbs[5 * third:])
    zb = [[zbs[(run * 2 + i) * third:(run * 2 + i + 1) * third] for i in (0, 1)] for run in (0, 1)]
    tok = q_ref.shape[0]
    arguments = (
        (q_in, q_ref), (g_in, g_ref), (k_in, k_ref), (v_in, v_ref), (wd_in, wd_ref), (o_in, o_ref), (lse_in, lse_ref),
    )
    loads = [pltpu.make_async_copy(src, dst, in_sem.at[i]) for i, (src, dst) in enumerate(arguments)]
    for load in loads:
        load.start()
    scale = hd ** -0.5
    row_ok = lambda step: (row + step >= 0) & (row + step < n_sh)
    col_ok = lambda step: (col + step >= 0) & (col + step < n_sw)
    spans = [(0, half - third + 1)] + [(half - third + k, half - third + k + 1) for k in range(1, third)]
    MESH = pl.DeviceIdType.MESH

    def sent_to(e):
        return row_ok(ROW_STEP[e % 3]) & col_ok(COL_STEP[e // 3])

    def came_from(e):
        return row_ok(-ROW_STEP[e % 3]) & col_ok(-COL_STEP[e // 3])

    def remote(src, dst, ssem, rsem, device):
        return pltpu.make_async_remote_copy(
            src_ref=src, dst_ref=dst, send_sem=ssem, recv_sem=rsem, device_id=device, device_id_type=MESH,
        )

    def copy_z(run, i, k, a):
        lo, hi = ((run * half + h) * hd for h in spans[k])
        src = (q_in, g_in)[a].at[:, lo:hi]
        return remote(src, zb[run][i][k].at[a], zs.at[i], zr.at[run, i, k], {"sh": row + 2 * i - 1})

    def copy_zstat(i):
        return remote(stats.at[6], stats.at[7 + i], zts.at[i], ztr.at[i], {"sh": row + 2 * i - 1})

    def copy_x(run, a):
        cols = slice(run * half * hd, (run + 1) * half * hd)
        return remote((k_in, v_in)[a].at[:, cols], kvx.at[a, :, cols], xs.at[0], xr.at[run], {"tp": 1 - part})

    def copy_w(run, e, k):
        return remote(
            packed.at[run, e, k], pieces[run][k].at[e], ws.at[e // 3], wr.at[run, e // 3, k], {"sw": col + COL_STEP[e // 3]},
        )

    def copy_wstat(e):
        return remote(stats.at[6 + e % 3], stats.at[e], wts.at[e // 3], wtr.at[e // 3], {"sw": col + COL_STEP[e // 3]})

    def copy_back(run, e, k):
        at = run * 9 + e
        home = {"sh": row - ROW_STEP[e % 3], "sw": col - COL_STEP[e // 3]}
        return remote(dqs.at[at, k], dqr[run].at[e * third + k], bs.at[e % 3], br.at[run, e % 3], home)

    def copy_xback(run, h):
        return remote(xsend.at[run, h], xback.at[run, h], xs.at[0], rxr.at[run], {"tp": 1 - part})

    n_rows = row_ok(-1).astype(jnp.int32) + row_ok(1).astype(jnp.int32)
    n_cols = col_ok(-1).astype(jnp.int32) + col_ok(1).astype(jnp.int32)

    def drain(ref, sem):
        pltpu.make_async_copy(ref, ref, sem).wait()

    barrier = pltpu.get_barrier_semaphore()
    pl.semaphore_signal(barrier, inc=1, device_id={"tp": 1 - part}, device_id_type=MESH)
    count = 1
    for e in SIDES:
        @pl.when(sent_to(e))
        def _():
            near = {"sh": row + ROW_STEP[e % 3], "sw": col + COL_STEP[e // 3]}
            pl.semaphore_signal(barrier, inc=1, device_id=near, device_id_type=MESH)
        count = count + sent_to(e).astype(jnp.int32)

    pl.semaphore_wait(barrier, count)

    def send_z(run):
        for k in range(third):
            for i in (0, 1):
                @pl.when(row_ok(2 * i - 1))
                def _():
                    copy_z(run, i, k, 0).start()
                    copy_z(run, i, k, 1).start()

    send_z(0)
    for run in (0, 1):
        for a in (0, 1):
            copy_x(run, a).start()

    for i in (4, 0, 1, 5, 6):
        loads[i].wait()
    for run in (0, 1):
        seen = jnp.int32(0)
        heads = [jnp.int32(0) for _ in range(third)]
        slots = [jnp.int32(0) for _ in range(third)]
        for h in range(half):
            dirs = [wd_ref[j, run * half + h] for j in range(4)]
            bits = [(d & 1, (d >> 1) & 1, d >> 2) for d in dirs]
            one = [(1 + 15 * a) * (1 + 255 * b) * (1 + 65535 * c) for a, b, c in bits]
            for j in range(4):
                field = seen & (one[j] * 15)
                here = [field == one[j] * s for s in range(third)]
                rank = sum(here[s].astype(jnp.int32) * s for s in range(1, third))
                n = dirs[j] + bits[j][2]
                up = (n * 11) >> 5
                over = n - 3 * up
                e = jnp.where(over == 1, 6, jnp.where(over == 2, 3, 0)) + jnp.where(up == 1, 0, jnp.where(up == 2, 2, 1))
                flat_of[(run * half + h) * 4 + j] = e * third + rank
                e_of[(run * half + h) * 4 + j] = e
                rank_of[(run * half + h) * 4 + j] = rank
                for s in range(third):
                    mine = jnp.where(here[s], one[j], 0)
                    if h:
                        heads[s] = heads[s] + mine * h
                    if j:
                        slots[s] = slots[s] + mine * j
            seen = seen + (one[0] + one[1]) + (one[2] + one[3])
        for d in range(8):
            for s in range(third):
                h = jnp.minimum(lax.shift_right_logical(heads[s], 4 * d) & 15, half - 1)
                head_of[(run * 9 + E_OF[d]) * third + s] = h
                src_of[(run * 9 + E_OF[d]) * third + s] = (run * half + h) * 4 + jnp.minimum(lax.shift_right_logical(slots[s], 4 * d) & 15, 3)

    lane = lax.broadcasted_iota(jnp.int32, (tok, hd), 1)
    table = jnp.zeros((tok, hd), F32)
    for at in range(2 * half):
        cols = slice(at * hd, (at + 1) * hd)
        delta = jnp.sum(g_ref[:, cols].astype(F32) * o_ref[:, cols].astype(F32), axis=1, keepdims=True)
        table = jnp.where(lane == at, lse_ref[:, at:at + 1], table)
        table = jnp.where(lane == 16 + at, delta, table)
    turned = jnp.concatenate([table, jnp.zeros((hd - tok, hd), F32)], axis=0).T
    stats[6] = turned[:16] + pltpu.roll(turned[16:32], tok, 1)
    for i in (0, 1):
        @pl.when(row_ok(2 * i - 1))
        def _():
            copy_zstat(i).start()
    send_z(1)

    def pack(run, e, s):
        i = e % 3
        h = head_of[(run * 9 + e) * third + s]
        block = zq[run * 2 + i - 1, h] if i else qg[run, h]
        if e // 3 == 2:
            pieces[run][s][e] = block
        else:
            packed[run, e, s] = block

    for run in (0, 1):
        for h in range(half):
            cols = slice((run * half + h) * hd, (run * half + h + 1) * hd)
            qg[run, h, 0] = q_ref[:, cols]
            qg[run, h, 1] = g_ref[:, cols]
    for run in (0, 1):
        for e in (0, 3):
            @pl.when(sent_to(e))
            def _():
                for s in range(third):
                    pack(run, e, s)
                    copy_w(run, e, s).start()
    for e in (0, 3):
        @pl.when(sent_to(e))
        def _():
            copy_wstat(e).start()

    for e in SIDES:
        @pl.when(jnp.logical_not(came_from(e)))
        def _():
            stats[e] = jnp.zeros(stats.shape[1:], F32)
            for run in (0, 1):
                for k in range(third):
                    pieces[run][k][e] = jnp.zeros(packed.shape[3:], BF)

        @pl.when(jnp.logical_not(sent_to(e)))
        def _():
            for run in (0, 1):
                dqr[run][e * third:(e + 1) * third] = jnp.zeros((third,) + dqr0.shape[1:], BF)

    def relay(run, k):
        for i in (1, 2):
            @pl.when(row_ok(-ROW_STEP[i]))
            def _():
                held = zb[run][i - 1][k]
                drain(held, zr.at[run, i - 1, k])
                for n, h in enumerate(range(*spans[k])):
                    for a in (0, 1):
                        zq[run * 2 + i - 1, h, a] = held[a, :, n * hd:(n + 1) * hd]
                if run == 0 and k == third - 1:
                    copy_zstat(i - 1).wait_recv()
                for e in (i, 3 + i):
                    @pl.when(col_ok(COL_STEP[e // 3]))
                    def _():
                        pack(run, e, k)
                        copy_w(run, e, k).start()
                        if run == 0 and k == third - 1:
                            copy_wstat(e).start()
                pack(run, 6 + i, k)

    def products(sets):
        scores = [lax.dot_general(keys, q, NT, preferred_element_type=F32) for keys, _, q, _, _, _ in sets]
        grad_prob = [lax.dot_general(vals, g, NT, preferred_element_type=F32) for _, vals, _, g, _, _ in sets]
        prob = [jnp.exp(score * scale - part[4]) for score, part in zip(scores, sets)]
        score_bf = [(p * (grad - part[5])).astype(BF) for p, grad, part in zip(prob, grad_prob, sets)]
        dv = [jnp.dot(p.astype(BF), part[3], preferred_element_type=F32) for p, part in zip(prob, sets)]
        dk = [jnp.dot(score, part[2], preferred_element_type=F32) * scale for score, part in zip(score_bf, sets)]
        dq = [lax.dot_general(score, part[0], TN, preferred_element_type=F32) * scale for score, part in zip(score_bf, sets)]
        return zip(dq, dk, dv)

    def keys_of(at):
        cols = slice(at * hd, (at + 1) * hd)
        return (jnp.concatenate([mine[:, cols], other[:, cols]], axis=0) for mine, other in ((k_ref, kvx.at[0]), (v_ref, kvx.at[1])))

    def own(run):
        for lo in range(0, half, 3):
            heads = range(run * half + lo, run * half + min(lo + 3, half))
            sets = []
            for at in heads:
                cols = slice(at * hd, (at + 1) * hd)
                stat = stats[6, at:at + 1, :]
                sets.append((*keys_of(at), q_ref[:, cols], g_ref[:, cols], stat[:, :tok], pltpu.roll(stat, tok, 1)[:, :tok]))
            for at, (dq, dk, dv) in zip(heads, products(sets)):
                own_q[at] = dq
                own_kv[at, 0] = dk
                own_kv[at, 1] = dv

    first = lax.broadcasted_iota(jnp.int32, (1, hd), 1) < tok

    def parts_of(run, h):
        at = run * half + h
        blocks = []
        for j in range(4):
            e = e_of[at * 4 + j]
            block = pieces[run][0][e]
            for k in range(1, min(h, third - 1) + 1):
                block = jnp.where(rank_of[at * 4 + j] == k, pieces[run][k][e], block)
            blocks.append(block)
        q = jnp.concatenate([block[0] for block in blocks], axis=0)
        g = jnp.concatenate([block[1] for block in blocks], axis=0)
        stat = [stats[e_of[at * 4 + j], at:at + 1, :] for j in range(4)]
        turn = [pltpu.roll(s, tok, 1) for s in stat]
        lse = jnp.concatenate([jnp.where(first, stat[j], turn[j + 1]) for j in (0, 2)], axis=1)
        delta = jnp.concatenate([jnp.where(first, turn[j], stat[j + 1]) for j in (0, 2)], axis=1)
        return (*keys_of(at), q, g, lse, delta)

    def arrived(run, k):
        for c in (0, 1):
            for v in (0, 1, 2):
                @pl.when(col_ok(-COL_STEP[c]) & (n_rows == v))
                def _():
                    drain(pieces[run][k].at[0:1 + v], wr.at[run, c, k])
                    if run == 0 and k == 0:
                        drain(stats.at[0:1 + v], wtr.at[c])

    def nears(run, *heads):
        for h, (dq, dk, dv) in zip(heads, products([parts_of(run, h) for h in heads])):
            at = run * half + h
            for a, grad in ((0, dk), (1, dv)):
                total = own_kv[at, a] + grad
                own_kv[at, a, :tok] = total[:tok]
                xsend[run, h, a] = total[tok:].astype(BF)
            for j in range(4):
                dqp[at * 4 + j] = dq[j * tok:(j + 1) * tok].astype(BF)
        for h in heads:
            copy_xback(run, h).start()

    def back(run, k, some=SIDES):
        for e in some:
            dqs[run * 9 + e, k] = dqp[src_of[(run * 9 + e) * third + k]]
        for e in some:
            @pl.when(came_from(e))
            def _():
                copy_back(run, e, k).start()

    def finish_kv(run):
        drain(xback.at[run], rxr.at[run])
        for h in range(half):
            cols = slice((run * half + h) * hd, (run * half + h + 1) * hd)
            for a, out in ((0, dk_out), (1, dv_out)):
                out[:, cols] = (own_kv[run * half + h, a, :tok] + xback[run, h, a].astype(F32)).astype(BF)

    def finish_q(run):
        for i in range(3):
            for v in (0, 1, 2):
                if v or i:
                    @pl.when(row_ok(ROW_STEP[i]) & (n_cols == v))
                    def _():
                        drain(dqr[run].at[0:third * (v + (i > 0))], br.at[run, i])
        for h in range(half):
            at = run * half + h
            total = own_q[at]
            for j in range(4):
                total = total + dqr[run][flat_of[at * 4 + j]].astype(F32)
            dq_out[:, at * hd:(at + 1) * hd] = total.astype(BF)

    def got_x(run):
        drain(kvx.at[:, :, run * half * hd:(run + 1) * half * hd], xr.at[run])

    loads[2].wait()
    loads[3].wait()
    relay(0, 0)
    relay(0, 1)
    relay(0, 2)
    got_x(0)
    own(0)
    arrived(0,0)
    nears(0,0)
    arrived(0,1)
    nears(0,1)
    relay(1,0)
    arrived(0,2)
    nears(0,2,3)
    relay(1,1)
    relay(1,2)
    nears(0,4,5)
    got_x(1)
    own(1)
    back(0,0,(7,8,1,2,4,5,0,3))
    back(0,1,(7,8,1,2,4,5,0,3))
    back(0,2,(7,8,1,2,4,5,0,3))
    arrived(1,0)
    nears(1,0)
    arrived(1,1)
    nears(1,1)
    arrived(1,2)
    nears(1,2,3,4,5)
    back(1,0,(1,2,4,5))
    back(1,1,(1,2,4,5))
    back(1,2,(1,2,4,5))
    back(1,0,(7,8))
    back(1,1,(7,8))
    back(1,2,(7,8))
    back(1,0,(0,3))
    back(1,1,(0,3))
    back(1,2,(0,3))
    finish_kv(0)
    finish_q(0)
    finish_kv(1)
    finish_q(1)

    drain(dqp, xs.at[0])
    for i in (0, 1):
        @pl.when(row_ok(2 * i - 1))
        def _():
            drain(dqp.at[0:4 * half], zs.at[i])
            copy_zstat(i).wait_send()
    for v in (0, 1, 2):
        for c in (0, 1):
            @pl.when(col_ok(COL_STEP[c]) & (n_rows == v))
            def _():
                drain(dqp.at[0:4 * third * (1 + v)], ws.at[c])
                drain(stats.at[0:1 + v], wts.at[c])
        for i in range(3):
            if v or i:
                @pl.when(row_ok(-ROW_STEP[i]) & (n_cols == v))
                def _():
                    drain(dqp.at[0:2 * third * (v + (i > 0))], bs.at[i])


def hand_out(a_in, b_in, c_in, a_out, b_out, c_out, out_sem):
    outs = [
        pltpu.make_async_copy(src, dst, out_sem.at[i])
        for i, (src, dst) in enumerate(((a_in, a_out), (b_in, b_out), (c_in, c_out)))
    ]
    for copy in outs:
        copy.start()
    for copy in outs:
        copy.wait()


def local(n_sh, n_sw, queries, keys, values, attn_out, attn_grad, log_sum, window_dirs):
    shape = queries.shape
    tok = shape[0] * shape[1] * shape[2]
    cols = shape[3]
    heads = log_sum.shape[3]
    half = heads // 2
    third = half // 2
    hd = cols // heads
    place = pltpu.with_memory_space_constraint
    flat = lambda array: place(array.reshape(tok, array.shape[3]), pltpu.HBM)
    vmem = pl.BlockSpec(memory_space=pltpu.VMEM)
    hbm = pl.BlockSpec(memory_space=pltpu.HBM)
    dma = pltpu.SemaphoreType.DMA
    scratch = (
        [
            pltpu.VMEM((2, tok, cols), BF),
            pltpu.VMEM((2, half, 2, tok, hd), BF),
            pltpu.VMEM((4, half, 2, tok, hd), BF),
        ]
        + [
            pltpu.VMEM((2, 6, third, 2, tok, hd), BF),
            pltpu.VMEM((9, 16, hd), F32),
        ]
        + [pltpu.VMEM((tok, cols), BF) for _ in range(5)]
        + [pltpu.VMEM((tok, heads), F32), pltpu.SMEM((4, heads), jnp.int32), dma((7,))]
        + [
            pltpu.VMEM((heads * 4, tok, hd), BF),
            pltpu.VMEM((18, third, tok, hd), BF),
            pltpu.VMEM((9 * third, tok, hd), BF),
            pltpu.VMEM((9 * third, tok, hd), BF),
            pltpu.VMEM((heads, 2, 2 * tok, hd), F32),
            pltpu.VMEM((heads, tok, hd), F32),
            pltpu.VMEM((2, half, 2, tok, hd), BF),
            pltpu.VMEM((2, half, 2, tok, hd), BF),
            pltpu.SMEM((18 * third,), jnp.int32),
            pltpu.SMEM((18 * third,), jnp.int32),
            pltpu.SMEM((heads * 4,), jnp.int32),
            pltpu.SMEM((heads * 4,), jnp.int32),
            pltpu.SMEM((heads * 4,), jnp.int32),
        ]
    )
    sems = ((2,), (2, 2, third), (2,), (2,), (1,), (2,), (2,), (2, 2, third), (2,), (2,), (3,), (2, 3), (2,))
    scratch += [dma(sem) for sem in sems]
    for _ in range(4):
        scratch += [pltpu.VMEM((2, tok, (half - third + 1 if k == 0 else 1) * hd), BF) for k in range(third)]
    scratch += [pltpu.VMEM((9, 2, tok, hd), BF) for _ in range(2 * third)]
    dq, dk, dv = pl.pallas_call(
        functools.partial(kernel, n_sh, n_sw, half, hd),
        out_shape=[pltpu.VMEM((tok, cols), BF)] * 3,
        in_specs=[hbm] * 7,
        out_specs=[vmem] * 3,
        scratch_shapes=scratch,
        compiler_params=pltpu.CompilerParams(
            collective_id=0, has_side_effects=True, vmem_limit_bytes=32 * 2**20
        ),
    )(flat(queries), flat(keys), flat(values), flat(attn_grad), flat(attn_out), flat(log_sum), place(window_dirs.T, pltpu.HBM))
    dq, dk, dv = pl.pallas_call(
        hand_out,
        out_shape=[jax.ShapeDtypeStruct((tok, cols), BF)] * 3,
        in_specs=[vmem] * 3,
        out_specs=[hbm] * 3,
        scratch_shapes=[dma((3,))],
    )(*(place(array, pltpu.VMEM) for array in (dq, dk, dv)))
    return tuple(array.reshape(shape) for array in (dq, dk, dv))


def solution(mesh):
    spec = P("tp", "sh", "sw", None)
    return jax.shard_map(
        functools.partial(local, mesh.shape["sh"], mesh.shape["sw"]),
        mesh=mesh,
        in_specs=(spec,) * 6 + (P(),),
        out_specs=(spec,) * 3,
        check_vma=False,
    )
```

```python
import functools

import jax
import jax.numpy as jnp
from jax import lax
from jax.experimental import pallas as pl
from jax.experimental.pallas import tpu as pltpu
from jax.sharding import PartitionSpec as P

E_OF = (1, 7, 4, 0, 3, 2, 8, 5)
BF = jnp.bfloat16
F32 = jnp.float32
NT = (((1,), (1,)), ((), ()))
TN = (((0,), (0,)), ((), ()))


SIDES = (0, 1, 2, 3, 4, 5, 7, 8)
ROW_STEP = (0, -1, 1)
COL_STEP = (-1, 1, 0)


def kernel(
    n_sh, n_sw, half, hd,
    q_in, k_in, v_in, g_in, o_in, lse_in, wd_in,
    dq_out, dk_out, dv_out,
    kvx, qg, zq, packed, stats,
    q_ref, k_ref, v_ref, g_ref, o_ref, lse_ref, wd_ref, in_sem,
    dqp, dqs, dqr0, dqr1, own_kv, own_q, xsend, xback,
    head_of, src_of, flat_of, e_of, rank_of,
    zs, zr, zts, ztr, xs, xr, ws, wr, wts, wtr, bs, br, rxr, *zbs,
):
    row = lax.axis_index("sh")
    col = lax.axis_index("sw")
    part = lax.axis_index("tp")
    dqr = (dqr0, dqr1)
    third = half // 2
    pieces = (zbs[4 * third:5 * third], zbs[5 * third:])
    zb = [[zbs[(run * 2 + i) * third:(run * 2 + i + 1) * third] for i in (0, 1)] for run in (0, 1)]
    tok = q_ref.shape[0]
    arguments = (
        (q_in, q_ref), (g_in, g_ref), (k_in, k_ref), (v_in, v_ref), (wd_in, wd_ref), (o_in, o_ref), (lse_in, lse_ref),
    )
    loads = [pltpu.make_async_copy(src, dst, in_sem.at[i]) for i, (src, dst) in enumerate(arguments)]
    scale = hd ** -0.5
    row_ok = lambda step: (row + step >= 0) & (row + step < n_sh)
    col_ok = lambda step: (col + step >= 0) & (col + step < n_sw)
    spans = [(0, half - third + 1)] + [(half - third + k, half - third + k + 1) for k in range(1, third)]
    MESH = pl.DeviceIdType.MESH

    def sent_to(e):
        return row_ok(ROW_STEP[e % 3]) & col_ok(COL_STEP[e // 3])

    def came_from(e):
        return row_ok(-ROW_STEP[e % 3]) & col_ok(-COL_STEP[e // 3])

    def remote(src, dst, ssem, rsem, device):
        return pltpu.make_async_remote_copy(
            src_ref=src, dst_ref=dst, send_sem=ssem, recv_sem=rsem, device_id=device, device_id_type=MESH,
        )

    def copy_z(run, i, k, a):
        lo, hi = ((run * half + h) * hd for h in spans[k])
        src = (q_in, g_in)[a].at[:, lo:hi]
        return remote(src, zb[run][i][k].at[a], zs.at[i], zr.at[run, i, k], {"sh": row + 2 * i - 1})

    def copy_zstat(i):
        return remote(stats.at[6], stats.at[7 + i], zts.at[i], ztr.at[i], {"sh": row + 2 * i - 1})

    def copy_x(run, a):
        cols = slice(run * half * hd, (run + 1) * half * hd)
        return remote((k_in, v_in)[a].at[:, cols], kvx.at[a, :, cols], xs.at[0], xr.at[run], {"tp": 1 - part})

    def copy_w(run, e, k):
        return remote(
            packed.at[run, e, k], pieces[run][k].at[e], ws.at[e // 3], wr.at[run, e // 3, k], {"sw": col + COL_STEP[e // 3]},
        )

    def copy_wstat(e):
        return remote(stats.at[6 + e % 3], stats.at[e], wts.at[e // 3], wtr.at[e // 3], {"sw": col + COL_STEP[e // 3]})

    def copy_back(run, e, k):
        at = run * 9 + e
        home = {"sh": row - ROW_STEP[e % 3], "sw": col - COL_STEP[e // 3]}
        return remote(dqs.at[at, k], dqr[run].at[e * third + k], bs.at[e % 3], br.at[run, e % 3], home)

    def copy_xback(run, h):
        return remote(xsend.at[run, h], xback.at[run, h], xs.at[0], rxr.at[run], {"tp": 1 - part})

    n_rows = row_ok(-1).astype(jnp.int32) + row_ok(1).astype(jnp.int32)
    n_cols = col_ok(-1).astype(jnp.int32) + col_ok(1).astype(jnp.int32)

    def drain(ref, sem):
        pltpu.make_async_copy(ref, ref, sem).wait()

    barrier = pltpu.get_barrier_semaphore()
    pl.semaphore_signal(barrier, inc=1, device_id={"tp": 1 - part}, device_id_type=MESH)
    count = 1
    for e in SIDES:
        @pl.when(sent_to(e))
        def _():
            near = {"sh": row + ROW_STEP[e % 3], "sw": col + COL_STEP[e // 3]}
            pl.semaphore_signal(barrier, inc=1, device_id=near, device_id_type=MESH)
        count = count + sent_to(e).astype(jnp.int32)

    for load in loads:
        load.start()
    pl.semaphore_wait(barrier, count)

    def send_z(run, *chunks):
        for k in chunks:
            for i in (0, 1):
                @pl.when(row_ok(2 * i - 1))
                def _():
                    copy_z(run, i, k, 0).start()
                    copy_z(run, i, k, 1).start()

    send_z(0, *range(third - 1))
    for run in (0, 1):
        for a in (0, 1):
            copy_x(run, a).start()

    for i in (4, 0, 1, 5, 6):
        loads[i].wait()
    for run in (0, 1):
        seen = jnp.int32(0)
        heads = [jnp.int32(0) for _ in range(third)]
        slots = [jnp.int32(0) for _ in range(third)]
        for h in range(half):
            dirs = [wd_ref[j, run * half + h] for j in range(4)]
            bits = [(d & 1, (d >> 1) & 1, d >> 2) for d in dirs]
            one = [(1 + 15 * a) * (1 + 255 * b) * (1 + 65535 * c) for a, b, c in bits]
            for j in range(4):
                field = seen & (one[j] * 15)
                here = [field == one[j] * s for s in range(third)]
                rank = sum(here[s].astype(jnp.int32) * s for s in range(1, third))
                n = dirs[j] + bits[j][2]
                up = (n * 11) >> 5
                over = n - 3 * up
                e = jnp.where(over == 1, 6, jnp.where(over == 2, 3, 0)) + jnp.where(up == 1, 0, jnp.where(up == 2, 2, 1))
                flat_of[(run * half + h) * 4 + j] = e * third + rank
                e_of[(run * half + h) * 4 + j] = e
                rank_of[(run * half + h) * 4 + j] = rank
                for s in range(third):
                    mine = jnp.where(here[s], one[j], 0)
                    if h:
                        heads[s] = heads[s] + mine * h
                    if j:
                        slots[s] = slots[s] + mine * j
            seen = seen + (one[0] + one[1]) + (one[2] + one[3])
        for d in range(8):
            for s in range(third):
                h = jnp.minimum(lax.shift_right_logical(heads[s], 4 * d) & 15, half - 1)
                head_of[(run * 9 + E_OF[d]) * third + s] = h
                src_of[(run * 9 + E_OF[d]) * third + s] = (run * half + h) * 4 + jnp.minimum(lax.shift_right_logical(slots[s], 4 * d) & 15, 3)

    lane = lax.broadcasted_iota(jnp.int32, (tok, hd), 1)
    table = jnp.zeros((tok, hd), F32)
    for at in range(2 * half):
        cols = slice(at * hd, (at + 1) * hd)
        delta = jnp.sum(g_ref[:, cols].astype(F32) * o_ref[:, cols].astype(F32), axis=1, keepdims=True)
        table = jnp.where(lane == at, lse_ref[:, at:at + 1], table)
        table = jnp.where(lane == 16 + at, delta, table)
    turned = jnp.concatenate([table, jnp.zeros((hd - tok, hd), F32)], axis=0).T
    stats[6] = turned[:16] + pltpu.roll(turned[16:32], tok, 1)
    for i in (0, 1):
        @pl.when(row_ok(2 * i - 1))
        def _():
            copy_zstat(i).start()
    send_z(0, third - 1)
    send_z(1, *range(third))

    def pack(run, e, s):
        i = e % 3
        h = head_of[(run * 9 + e) * third + s]
        block = zq[run * 2 + i - 1, h] if i else qg[run, h]
        if e // 3 == 2:
            pieces[run][s][e] = block
        else:
            packed[run, e, s] = block

    for run in (0, 1):
        for h in range(half):
            cols = slice((run * half + h) * hd, (run * half + h + 1) * hd)
            qg[run, h, 0] = q_ref[:, cols]
            qg[run, h, 1] = g_ref[:, cols]
    for run in (0, 1):
        for e in (0, 3):
            @pl.when(sent_to(e))
            def _():
                for s in range(third):
                    pack(run, e, s)
                    copy_w(run, e, s).start()
    for e in (0, 3):
        @pl.when(sent_to(e))
        def _():
            copy_wstat(e).start()

    for e in SIDES:
        @pl.when(jnp.logical_not(came_from(e)))
        def _():
            stats[e] = jnp.zeros(stats.shape[1:], F32)
            for run in (0, 1):
                for k in range(third):
                    pieces[run][k][e] = jnp.zeros(packed.shape[3:], BF)

        @pl.when(jnp.logical_not(sent_to(e)))
        def _():
            for run in (0, 1):
                dqr[run][e * third:(e + 1) * third] = jnp.zeros((third,) + dqr0.shape[1:], BF)

    def relay(run, k):
        for i in (1, 2):
            @pl.when(row_ok(-ROW_STEP[i]))
            def _():
                held = zb[run][i - 1][k]
                drain(held, zr.at[run, i - 1, k])
                for n, h in enumerate(range(*spans[k])):
                    for a in (0, 1):
                        zq[run * 2 + i - 1, h, a] = held[a, :, n * hd:(n + 1) * hd]
                if run == 0 and k == third - 2:
                    copy_zstat(i - 1).wait_recv()
                for e in (i, 3 + i):
                    @pl.when(col_ok(COL_STEP[e // 3]))
                    def _():
                        pack(run, e, k)
                        copy_w(run, e, k).start()
                        if run == 0 and k == third - 2:
                            copy_wstat(e).start()
                pack(run, 6 + i, k)

    def products(sets):
        scores = [lax.dot_general(keys, q, NT, preferred_element_type=F32) for keys, _, q, _, _, _ in sets]
        grad_prob = [lax.dot_general(vals, g, NT, preferred_element_type=F32) for _, vals, _, g, _, _ in sets]
        prob = [jnp.exp(score * scale - part[4]) for score, part in zip(scores, sets)]
        score_bf = [(p * (grad - part[5])).astype(BF) for p, grad, part in zip(prob, grad_prob, sets)]
        dv = [jnp.dot(p.astype(BF), part[3], preferred_element_type=F32) for p, part in zip(prob, sets)]
        dk = [jnp.dot(score, part[2], preferred_element_type=F32) * scale for score, part in zip(score_bf, sets)]
        dq = [lax.dot_general(score, part[0], TN, preferred_element_type=F32) * scale for score, part in zip(score_bf, sets)]
        return zip(dq, dk, dv)

    def keys_of(at):
        cols = slice(at * hd, (at + 1) * hd)
        return (jnp.concatenate([mine[:, cols], other[:, cols]], axis=0) for mine, other in ((k_ref, kvx.at[0]), (v_ref, kvx.at[1])))

    def own(run):
        for lo in range(0, half, 3):
            heads = range(run * half + lo, run * half + min(lo + 3, half))
            sets = []
            for at in heads:
                cols = slice(at * hd, (at + 1) * hd)
                stat = stats[6, at:at + 1, :]
                sets.append((*keys_of(at), q_ref[:, cols], g_ref[:, cols], stat[:, :tok], pltpu.roll(stat, tok, 1)[:, :tok]))
            for at, (dq, dk, dv) in zip(heads, products(sets)):
                own_q[at] = dq
                own_kv[at, 0] = dk
                own_kv[at, 1] = dv

    first = lax.broadcasted_iota(jnp.int32, (1, hd), 1) < tok

    def parts_of(run, h):
        at = run * half + h
        blocks = []
        for j in range(4):
            e = e_of[at * 4 + j]
            block = pieces[run][0][e]
            for k in range(1, min(h, third - 1) + 1):
                block = jnp.where(rank_of[at * 4 + j] == k, pieces[run][k][e], block)
            blocks.append(block)
        q = jnp.concatenate([block[0] for block in blocks], axis=0)
        g = jnp.concatenate([block[1] for block in blocks], axis=0)
        stat = [stats[e_of[at * 4 + j], at:at + 1, :] for j in range(4)]
        turn = [pltpu.roll(s, tok, 1) for s in stat]
        lse = jnp.concatenate([jnp.where(first, stat[j], turn[j + 1]) for j in (0, 2)], axis=1)
        delta = jnp.concatenate([jnp.where(first, turn[j], stat[j + 1]) for j in (0, 2)], axis=1)
        return (*keys_of(at), q, g, lse, delta)

    def arrived(run, k):
        for c in (0, 1):
            for v in (0, 1, 2):
                @pl.when(col_ok(-COL_STEP[c]) & (n_rows == v))
                def _():
                    drain(pieces[run][k].at[0:1 + v], wr.at[run, c, k])
                    if run == 0 and k == 0:
                        drain(stats.at[0:1 + v], wtr.at[c])

    def nears(run, *heads):
        for h, (dq, dk, dv) in zip(heads, products([parts_of(run, h) for h in heads])):
            at = run * half + h
            for a, grad in ((0, dk), (1, dv)):
                total = own_kv[at, a] + grad
                own_kv[at, a, :tok] = total[:tok]
                xsend[run, h, a] = total[tok:].astype(BF)
            for j in range(4):
                dqp[at * 4 + j] = dq[j * tok:(j + 1) * tok].astype(BF)
        for h in heads:
            copy_xback(run, h).start()

    def back(run, k, some=SIDES):
        for e in some:
            dqs[run * 9 + e, k] = dqp[src_of[(run * 9 + e) * third + k]]
        for e in some:
            @pl.when(came_from(e))
            def _():
                copy_back(run, e, k).start()

    def finish_kv(run):
        drain(xback.at[run], rxr.at[run])
        for h in range(half):
            cols = slice((run * half + h) * hd, (run * half + h + 1) * hd)
            for a, out in ((0, dk_out), (1, dv_out)):
                out[:, cols] = (own_kv[run * half + h, a, :tok] + xback[run, h, a].astype(F32)).astype(BF)

    def finish_q(run):
        for i in range(3):
            for v in (0, 1, 2):
                if v or i:
                    @pl.when(row_ok(ROW_STEP[i]) & (n_cols == v))
                    def _():
                        drain(dqr[run].at[0:third * (v + (i > 0))], br.at[run, i])
        for h in range(half):
            at = run * half + h
            total = own_q[at]
            for j in range(4):
                total = total + dqr[run][flat_of[at * 4 + j]].astype(F32)
            dq_out[:, at * hd:(at + 1) * hd] = total.astype(BF)

    def got_x(run):
        drain(kvx.at[:, :, run * half * hd:(run + 1) * half * hd], xr.at[run])

    loads[2].wait()
    loads[3].wait()
    relay(0, 0)
    relay(0, 1)
    relay(0, 2)
    got_x(0)
    own(0)
    arrived(0,0)
    nears(0,0)
    arrived(0,1)
    nears(0,1)
    relay(1,0)
    arrived(0,2)
    nears(0,2,3)
    relay(1,1)
    relay(1,2)
    nears(0,4,5)
    got_x(1)
    own(1)
    back(0,0,(7,8,1,2,4,5,0,3))
    back(0,1,(7,8,1,2,4,5,0,3))
    back(0,2,(7,8,1,2,4,5,0,3))
    arrived(1,0)
    nears(1,0)
    arrived(1,1)
    nears(1,1)
    arrived(1,2)
    nears(1,2,3,4,5)
    back(1,0,(1,2,4,5))
    back(1,1,(1,2,4,5))
    back(1,2,(1,2,4,5))
    back(1,0,(7,8))
    back(1,1,(7,8))
    back(1,2,(7,8))
    back(1,0,(0,3))
    back(1,1,(0,3))
    back(1,2,(0,3))
    finish_kv(0)
    finish_q(0)
    finish_kv(1)
    finish_q(1)

    drain(dqp, xs.at[0])
    for i in (0, 1):
        @pl.when(row_ok(2 * i - 1))
        def _():
            drain(dqp.at[0:4 * half], zs.at[i])
            copy_zstat(i).wait_send()
    for v in (0, 1, 2):
        for c in (0, 1):
            @pl.when(col_ok(COL_STEP[c]) & (n_rows == v))
            def _():
                drain(dqp.at[0:4 * third * (1 + v)], ws.at[c])
                drain(stats.at[0:1 + v], wts.at[c])
        for i in range(3):
            if v or i:
                @pl.when(row_ok(-ROW_STEP[i]) & (n_cols == v))
                def _():
                    drain(dqp.at[0:2 * third * (v + (i > 0))], bs.at[i])


def hand_out(a_in, b_in, c_in, a_out, b_out, c_out, out_sem):
    outs = [
        pltpu.make_async_copy(src, dst, out_sem.at[i])
        for i, (src, dst) in enumerate(((a_in, a_out), (b_in, b_out), (c_in, c_out)))
    ]
    for copy in outs:
        copy.start()
    for copy in outs:
        copy.wait()


def local(n_sh, n_sw, queries, keys, values, attn_out, attn_grad, log_sum, window_dirs):
    shape = queries.shape
    tok = shape[0] * shape[1] * shape[2]
    cols = shape[3]
    heads = log_sum.shape[3]
    half = heads // 2
    third = half // 2
    hd = cols // heads
    place = pltpu.with_memory_space_constraint
    flat = lambda array: place(array.reshape(tok, array.shape[3]), pltpu.HBM)
    vmem = pl.BlockSpec(memory_space=pltpu.VMEM)
    hbm = pl.BlockSpec(memory_space=pltpu.HBM)
    dma = pltpu.SemaphoreType.DMA
    scratch = (
        [
            pltpu.VMEM((2, tok, cols), BF),
            pltpu.VMEM((2, half, 2, tok, hd), BF),
            pltpu.VMEM((4, half, 2, tok, hd), BF),
        ]
        + [
            pltpu.VMEM((2, 6, third, 2, tok, hd), BF),
            pltpu.VMEM((9, 16, hd), F32),
        ]
        + [pltpu.VMEM((tok, cols), BF) for _ in range(5)]
        + [pltpu.VMEM((tok, heads), F32), pltpu.SMEM((4, heads), jnp.int32), dma((7,))]
        + [
            pltpu.VMEM((heads * 4, tok, hd), BF),
            pltpu.VMEM((18, third, tok, hd), BF),
            pltpu.VMEM((9 * third, tok, hd), BF),
            pltpu.VMEM((9 * third, tok, hd), BF),
            pltpu.VMEM((heads, 2, 2 * tok, hd), F32),
            pltpu.VMEM((heads, tok, hd), F32),
            pltpu.VMEM((2, half, 2, tok, hd), BF),
            pltpu.VMEM((2, half, 2, tok, hd), BF),
            pltpu.SMEM((18 * third,), jnp.int32),
            pltpu.SMEM((18 * third,), jnp.int32),
            pltpu.SMEM((heads * 4,), jnp.int32),
            pltpu.SMEM((heads * 4,), jnp.int32),
            pltpu.SMEM((heads * 4,), jnp.int32),
        ]
    )
    sems = ((2,), (2, 2, third), (2,), (2,), (1,), (2,), (2,), (2, 2, third), (2,), (2,), (3,), (2, 3), (2,))
    scratch += [dma(sem) for sem in sems]
    for _ in range(4):
        scratch += [pltpu.VMEM((2, tok, (half - third + 1 if k == 0 else 1) * hd), BF) for k in range(third)]
    scratch += [pltpu.VMEM((9, 2, tok, hd), BF) for _ in range(2 * third)]
    dq, dk, dv = pl.pallas_call(
        functools.partial(kernel, n_sh, n_sw, half, hd),
        out_shape=[pltpu.VMEM((tok, cols), BF)] * 3,
        in_specs=[hbm] * 7,
        out_specs=[vmem] * 3,
        scratch_shapes=scratch,
        compiler_params=pltpu.CompilerParams(
            collective_id=0, has_side_effects=True, vmem_limit_bytes=32 * 2**20
        ),
    )(flat(queries), flat(keys), flat(values), flat(attn_grad), flat(attn_out), flat(log_sum), place(window_dirs.T, pltpu.HBM))
    dq, dk, dv = pl.pallas_call(
        hand_out,
        out_shape=[jax.ShapeDtypeStruct((tok, cols), BF)] * 3,
        in_specs=[vmem] * 3,
        out_specs=[hbm] * 3,
        scratch_shapes=[dma((3,))],
    )(*(place(array, pltpu.VMEM) for array in (dq, dk, dv)))
    return tuple(array.reshape(shape) for array in (dq, dk, dv))


def solution(mesh):
    spec = P("tp", "sh", "sw", None)
    return jax.shard_map(
        functools.partial(local, mesh.shape["sh"], mesh.shape["sw"]),
        mesh=mesh,
        in_specs=(spec,) * 6 + (P(),),
        out_specs=(spec,) * 3,
        check_vma=False,
    )
```

```python
import functools

import jax
import jax.numpy as jnp
from jax import lax
from jax.experimental import pallas as pl
from jax.experimental.pallas import tpu as pltpu
from jax.sharding import PartitionSpec as P

E_OF = (1, 7, 4, 0, 3, 2, 8, 5)
BF = jnp.bfloat16
F32 = jnp.float32
NT = (((1,), (1,)), ((), ()))
TN = (((0,), (0,)), ((), ()))


SIDES = (0, 1, 2, 3, 4, 5, 7, 8)
ROW_STEP = (0, -1, 1)
COL_STEP = (-1, 1, 0)


def kernel(
    n_sh, n_sw, half, hd,
    q_in, k_in, v_in, g_in, o_in, lse_in, wd_in,
    dq_out, dk_out, dv_out,
    kvx, qg, zq, packed, stats,
    q_ref, k_ref, v_ref, g_ref, o_ref, lse_ref, wd_ref, in_sem,
    dqp, dqs, dqr0, dqr1, own_kv, own_q, xsend, xback,
    head_of, src_of, flat_of, e_of, rank_of,
    zs, zr, zts, ztr, xs, xr, ws, wr, wts, wtr, bs, br, rxr, *zbs,
):
    row = lax.axis_index("sh")
    col = lax.axis_index("sw")
    part = lax.axis_index("tp")
    dqr = (dqr0, dqr1)
    third = half // 2
    pieces = (zbs[4 * third:5 * third], zbs[5 * third:])
    zb = [[zbs[(run * 2 + i) * third:(run * 2 + i + 1) * third] for i in (0, 1)] for run in (0, 1)]
    tok = q_ref.shape[0]
    arguments = (
        (q_in, q_ref), (g_in, g_ref), (k_in, k_ref), (v_in, v_ref), (wd_in, wd_ref), (o_in, o_ref), (lse_in, lse_ref),
    )
    loads = [pltpu.make_async_copy(src, dst, in_sem.at[i]) for i, (src, dst) in enumerate(arguments)]
    scale = hd ** -0.5
    row_ok = lambda step: (row + step >= 0) & (row + step < n_sh)
    col_ok = lambda step: (col + step >= 0) & (col + step < n_sw)
    spans = [(0, half - third + 1)] + [(half - third + k, half - third + k + 1) for k in range(1, third)]
    MESH = pl.DeviceIdType.MESH

    def sent_to(e):
        return row_ok(ROW_STEP[e % 3]) & col_ok(COL_STEP[e // 3])

    def came_from(e):
        return row_ok(-ROW_STEP[e % 3]) & col_ok(-COL_STEP[e // 3])

    def remote(src, dst, ssem, rsem, device):
        return pltpu.make_async_remote_copy(
            src_ref=src, dst_ref=dst, send_sem=ssem, recv_sem=rsem, device_id=device, device_id_type=MESH,
        )

    def copy_z(run, i, k, a):
        lo, hi = ((run * half + h) * hd for h in spans[k])
        src = (q_in, g_in)[a].at[:, lo:hi]
        return remote(src, zb[run][i][k].at[a], zs.at[i], zr.at[run, i, k], {"sh": row + 2 * i - 1})

    def copy_zstat(i):
        return remote(stats.at[6], stats.at[7 + i], zts.at[i], ztr.at[i], {"sh": row + 2 * i - 1})

    def copy_x(run, a):
        cols = slice(run * half * hd, (run + 1) * half * hd)
        return remote((k_in, v_in)[a].at[:, cols], kvx.at[a, :, cols], xs.at[0], xr.at[run], {"tp": 1 - part})

    def copy_w(run, e, k):
        return remote(
            packed.at[run, e, k], pieces[run][k].at[e], ws.at[e // 3], wr.at[run, e // 3, k], {"sw": col + COL_STEP[e // 3]},
        )

    def copy_wstat(e):
        return remote(stats.at[6 + e % 3], stats.at[e], wts.at[e // 3], wtr.at[e // 3], {"sw": col + COL_STEP[e // 3]})

    def copy_back(run, e, k):
        at = run * 9 + e
        home = {"sh": row - ROW_STEP[e % 3], "sw": col - COL_STEP[e // 3]}
        return remote(dqs.at[at, k], dqr[run].at[e * third + k], bs.at[e % 3], br.at[run, e % 3], home)

    def copy_xback(run, h):
        return remote(xsend.at[run, h], xback.at[run, h], xs.at[0], rxr.at[run, int(h >= half - 1)], {"tp": 1 - part})

    n_rows = row_ok(-1).astype(jnp.int32) + row_ok(1).astype(jnp.int32)
    n_cols = col_ok(-1).astype(jnp.int32) + col_ok(1).astype(jnp.int32)

    def drain(ref, sem):
        pltpu.make_async_copy(ref, ref, sem).wait()

    barrier = pltpu.get_barrier_semaphore()
    pl.semaphore_signal(barrier, inc=1, device_id={"tp": 1 - part}, device_id_type=MESH)
    count = 1
    for e in SIDES:
        @pl.when(sent_to(e))
        def _():
            near = {"sh": row + ROW_STEP[e % 3], "sw": col + COL_STEP[e // 3]}
            pl.semaphore_signal(barrier, inc=1, device_id=near, device_id_type=MESH)
        count = count + sent_to(e).astype(jnp.int32)

    for load in loads:
        load.start()
    pl.semaphore_wait(barrier, count)

    def send_z(run, *chunks):
        for k in chunks:
            for i in (0, 1):
                @pl.when(row_ok(2 * i - 1))
                def _():
                    copy_z(run, i, k, 0).start()
                    copy_z(run, i, k, 1).start()

    send_z(0, *range(third - 1))
    for run in (0, 1):
        for a in (0, 1):
            copy_x(run, a).start()

    for i in (4, 0, 1, 5, 6):
        loads[i].wait()
    for run in (0, 1):
        seen = jnp.int32(0)
        heads = [jnp.int32(0) for _ in range(third)]
        slots = [jnp.int32(0) for _ in range(third)]
        for h in range(half):
            dirs = [wd_ref[j, run * half + h] for j in range(4)]
            bits = [(d & 1, (d >> 1) & 1, d >> 2) for d in dirs]
            one = [(1 + 15 * a) * (1 + 255 * b) * (1 + 65535 * c) for a, b, c in bits]
            for j in range(4):
                field = seen & (one[j] * 15)
                here = [field == one[j] * s for s in range(third)]
                rank = sum(here[s].astype(jnp.int32) * s for s in range(1, third))
                n = dirs[j] + bits[j][2]
                up = (n * 11) >> 5
                over = n - 3 * up
                e = jnp.where(over == 1, 6, jnp.where(over == 2, 3, 0)) + jnp.where(up == 1, 0, jnp.where(up == 2, 2, 1))
                flat_of[(run * half + h) * 4 + j] = e * third + rank
                e_of[(run * half + h) * 4 + j] = e
                rank_of[(run * half + h) * 4 + j] = rank
                for s in range(third):
                    mine = jnp.where(here[s], one[j], 0)
                    if h:
                        heads[s] = heads[s] + mine * h
                    if j:
                        slots[s] = slots[s] + mine * j
            seen = seen + (one[0] + one[1]) + (one[2] + one[3])
        for d in range(8):
            for s in range(third):
                h = jnp.minimum(lax.shift_right_logical(heads[s], 4 * d) & 15, half - 1)
                head_of[(run * 9 + E_OF[d]) * third + s] = h
                src_of[(run * 9 + E_OF[d]) * third + s] = (run * half + h) * 4 + jnp.minimum(lax.shift_right_logical(slots[s], 4 * d) & 15, 3)

    lane = lax.broadcasted_iota(jnp.int32, (tok, hd), 1)
    table = jnp.zeros((tok, hd), F32)
    for at in range(2 * half):
        cols = slice(at * hd, (at + 1) * hd)
        delta = jnp.sum(g_ref[:, cols].astype(F32) * o_ref[:, cols].astype(F32), axis=1, keepdims=True)
        table = jnp.where(lane == at, lse_ref[:, at:at + 1], table)
        table = jnp.where(lane == 16 + at, delta, table)
    turned = jnp.concatenate([table, jnp.zeros((hd - tok, hd), F32)], axis=0).T
    stats[6] = turned[:16] + pltpu.roll(turned[16:32], tok, 1)
    for i in (0, 1):
        @pl.when(row_ok(2 * i - 1))
        def _():
            copy_zstat(i).start()
    send_z(0, third - 1)
    send_z(1, *range(third))

    def pack(run, e, s):
        i = e % 3
        h = head_of[(run * 9 + e) * third + s]
        block = zq[run * 2 + i - 1, h] if i else qg[run, h]
        if e // 3 == 2:
            pieces[run][s][e] = block
        else:
            packed[run, e, s] = block

    for run in (0, 1):
        for h in range(half):
            cols = slice((run * half + h) * hd, (run * half + h + 1) * hd)
            qg[run, h, 0] = q_ref[:, cols]
            qg[run, h, 1] = g_ref[:, cols]
    for run in (0, 1):
        for e in (0, 3):
            @pl.when(sent_to(e))
            def _():
                for s in range(third):
                    pack(run, e, s)
                    copy_w(run, e, s).start()
    for e in (0, 3):
        @pl.when(sent_to(e))
        def _():
            copy_wstat(e).start()

    for e in SIDES:
        @pl.when(jnp.logical_not(came_from(e)))
        def _():
            stats[e] = jnp.zeros(stats.shape[1:], F32)
            for run in (0, 1):
                for k in range(third):
                    pieces[run][k][e] = jnp.zeros(packed.shape[3:], BF)

        @pl.when(jnp.logical_not(sent_to(e)))
        def _():
            for run in (0, 1):
                dqr[run][e * third:(e + 1) * third] = jnp.zeros((third,) + dqr0.shape[1:], BF)

    def relay(run, k):
        for i in (1, 2):
            @pl.when(row_ok(-ROW_STEP[i]))
            def _():
                held = zb[run][i - 1][k]
                drain(held, zr.at[run, i - 1, k])
                for n, h in enumerate(range(*spans[k])):
                    for a in (0, 1):
                        zq[run * 2 + i - 1, h, a] = held[a, :, n * hd:(n + 1) * hd]
                if run == 0 and k == third - 2:
                    copy_zstat(i - 1).wait_recv()
                for e in (i, 3 + i):
                    @pl.when(col_ok(COL_STEP[e // 3]))
                    def _():
                        pack(run, e, k)
                        copy_w(run, e, k).start()
                        if run == 0 and k == third - 2:
                            copy_wstat(e).start()
        for i in (1, 2):
            @pl.when(row_ok(-ROW_STEP[i]))
            def _():
                pack(run, 6 + i, k)

    def products(sets):
        scores = [lax.dot_general(keys, q, NT, preferred_element_type=F32) for keys, _, q, _, _, _ in sets]
        grad_prob = [lax.dot_general(vals, g, NT, preferred_element_type=F32) for _, vals, _, g, _, _ in sets]
        prob = [jnp.exp(score * scale - part[4]) for score, part in zip(scores, sets)]
        score_bf = [(p * (grad - part[5])).astype(BF) for p, grad, part in zip(prob, grad_prob, sets)]
        dv = [jnp.dot(p.astype(BF), part[3], preferred_element_type=F32) for p, part in zip(prob, sets)]
        dk = [jnp.dot(score, part[2], preferred_element_type=F32) * scale for score, part in zip(score_bf, sets)]
        dq = [lax.dot_general(score, part[0], TN, preferred_element_type=F32) * scale for score, part in zip(score_bf, sets)]
        return zip(dq, dk, dv)

    def keys_of(at):
        cols = slice(at * hd, (at + 1) * hd)
        return (jnp.concatenate([mine[:, cols], other[:, cols]], axis=0) for mine, other in ((k_ref, kvx.at[0]), (v_ref, kvx.at[1])))

    def own(run):
        for lo in range(0, half, 3):
            heads = range(run * half + lo, run * half + min(lo + 3, half))
            sets = []
            for at in heads:
                cols = slice(at * hd, (at + 1) * hd)
                stat = stats[6, at:at + 1, :]
                sets.append((*keys_of(at), q_ref[:, cols], g_ref[:, cols], stat[:, :tok], pltpu.roll(stat, tok, 1)[:, :tok]))
            for at, (dq, dk, dv) in zip(heads, products(sets)):
                own_q[at] = dq
                own_kv[at, 0] = dk
                own_kv[at, 1] = dv

    first = lax.broadcasted_iota(jnp.int32, (1, hd), 1) < tok

    def parts_of(run, h):
        at = run * half + h
        blocks = []
        for j in range(4):
            e = e_of[at * 4 + j]
            block = pieces[run][0][e]
            for k in range(1, min(h, third - 1) + 1):
                block = jnp.where(rank_of[at * 4 + j] == k, pieces[run][k][e], block)
            blocks.append(block)
        q = jnp.concatenate([block[0] for block in blocks], axis=0)
        g = jnp.concatenate([block[1] for block in blocks], axis=0)
        stat = [stats[e_of[at * 4 + j], at:at + 1, :] for j in range(4)]
        turn = [pltpu.roll(s, tok, 1) for s in stat]
        lse = jnp.concatenate([jnp.where(first, stat[j], turn[j + 1]) for j in (0, 2)], axis=1)
        delta = jnp.concatenate([jnp.where(first, turn[j], stat[j + 1]) for j in (0, 2)], axis=1)
        return (*keys_of(at), q, g, lse, delta)

    def arrived(run, k):
        for c in (0, 1):
            for v in (0, 1, 2):
                @pl.when(col_ok(-COL_STEP[c]) & (n_rows == v))
                def _():
                    drain(pieces[run][k].at[0:1 + v], wr.at[run, c, k])
                    if run == 0 and k == 0:
                        drain(stats.at[0:1 + v], wtr.at[c])

    def nears(run, *heads):
        for h, (dq, dk, dv) in zip(heads, products([parts_of(run, h) for h in heads])):
            at = run * half + h
            for a, grad in ((0, dk), (1, dv)):
                total = own_kv[at, a] + grad
                own_kv[at, a, :tok] = total[:tok]
                xsend[run, h, a] = total[tok:].astype(BF)
            for j in range(4):
                dqp[at * 4 + j] = dq[j * tok:(j + 1) * tok].astype(BF)
        for h in heads:
            copy_xback(run, h).start()

    def back(run, k, some=SIDES):
        for e in some:
            dqs[run * 9 + e, k] = dqp[src_of[(run * 9 + e) * third + k]]
        for e in some:
            @pl.when(came_from(e))
            def _():
                copy_back(run, e, k).start()

    def finish_kv(run):
        drain(xback.at[run, 0:half - 1], rxr.at[run, 0])
        for h in range(half):
            if h == half - 1:
                drain(xback.at[run, h], rxr.at[run, 1])
            cols = slice((run * half + h) * hd, (run * half + h + 1) * hd)
            for a, out in ((0, dk_out), (1, dv_out)):
                out[:, cols] = (own_kv[run * half + h, a, :tok] + xback[run, h, a].astype(F32)).astype(BF)

    def finish_q(run):
        for i in range(3):
            for v in (0, 1, 2):
                if v or i:
                    @pl.when(row_ok(ROW_STEP[i]) & (n_cols == v))
                    def _():
                        drain(dqr[run].at[0:third * (v + (i > 0))], br.at[run, i])
        for h in range(half):
            at = run * half + h
            total = own_q[at]
            for j in range(4):
                total = total + dqr[run][flat_of[at * 4 + j]].astype(F32)
            dq_out[:, at * hd:(at + 1) * hd] = total.astype(BF)

    def got_x(run):
        drain(kvx.at[:, :, run * half * hd:(run + 1) * half * hd], xr.at[run])

    loads[2].wait()
    loads[3].wait()
    relay(0, 0)
    relay(0, 1)
    relay(0, 2)
    got_x(0)
    own(0)
    arrived(0,0)
    nears(0,0)
    arrived(0,1)
    nears(0,1)
    relay(1,0)
    arrived(0,2)
    nears(0,2,3)
    relay(1,1)
    relay(1,2)
    nears(0,4,5)
    got_x(1)
    own(1)
    back(0,0,(7,8,1,2,4,5,0,3))
    back(0,1,(7,8,1,2,4,5,0,3))
    back(0,2,(7,8,1,2,4,5,0,3))
    arrived(1,0)
    nears(1,0)
    arrived(1,1)
    nears(1,1)
    arrived(1,2)
    nears(1,2,3,4,5)
    back(1,0,(1,2,4,5))
    back(1,1,(1,2,4,5))
    back(1,2,(1,2,4,5))
    back(1,0,(7,8))
    back(1,1,(7,8))
    back(1,2,(7,8))
    back(1,0,(0,3))
    back(1,1,(0,3))
    back(1,2,(0,3))
    finish_kv(0)
    finish_q(0)
    finish_q(1)
    finish_kv(1)

    drain(dqp, xs.at[0])
    for i in (0, 1):
        @pl.when(row_ok(2 * i - 1))
        def _():
            drain(dqp.at[0:4 * half], zs.at[i])
            copy_zstat(i).wait_send()
    for v in (0, 1, 2):
        for c in (0, 1):
            @pl.when(col_ok(COL_STEP[c]) & (n_rows == v))
            def _():
                drain(dqp.at[0:4 * third * (1 + v)], ws.at[c])
                drain(stats.at[0:1 + v], wts.at[c])
        for i in range(3):
            if v or i:
                @pl.when(row_ok(-ROW_STEP[i]) & (n_cols == v))
                def _():
                    drain(dqp.at[0:2 * third * (v + (i > 0))], bs.at[i])


def hand_out(a_in, b_in, c_in, a_out, b_out, c_out, out_sem):
    outs = [
        pltpu.make_async_copy(src, dst, out_sem.at[i])
        for i, (src, dst) in enumerate(((a_in, a_out), (b_in, b_out), (c_in, c_out)))
    ]
    for copy in outs:
        copy.start()
    for copy in outs:
        copy.wait()


def local(n_sh, n_sw, queries, keys, values, attn_out, attn_grad, log_sum, window_dirs):
    shape = queries.shape
    tok = shape[0] * shape[1] * shape[2]
    cols = shape[3]
    heads = log_sum.shape[3]
    half = heads // 2
    third = half // 2
    hd = cols // heads
    place = pltpu.with_memory_space_constraint
    flat = lambda array: place(array.reshape(tok, array.shape[3]), pltpu.HBM)
    vmem = pl.BlockSpec(memory_space=pltpu.VMEM)
    hbm = pl.BlockSpec(memory_space=pltpu.HBM)
    dma = pltpu.SemaphoreType.DMA
    scratch = (
        [
            pltpu.VMEM((2, tok, cols), BF),
            pltpu.VMEM((2, half, 2, tok, hd), BF),
            pltpu.VMEM((4, half, 2, tok, hd), BF),
        ]
        + [
            pltpu.VMEM((2, 6, third, 2, tok, hd), BF),
            pltpu.VMEM((9, 16, hd), F32),
        ]
        + [pltpu.VMEM((tok, cols), BF) for _ in range(5)]
        + [pltpu.VMEM((tok, heads), F32), pltpu.SMEM((4, heads), jnp.int32), dma((7,))]
        + [
            pltpu.VMEM((heads * 4, tok, hd), BF),
            pltpu.VMEM((18, third, tok, hd), BF),
            pltpu.VMEM((9 * third, tok, hd), BF),
            pltpu.VMEM((9 * third, tok, hd), BF),
            pltpu.VMEM((heads, 2, 2 * tok, hd), F32),
            pltpu.VMEM((heads, tok, hd), F32),
            pltpu.VMEM((2, half, 2, tok, hd), BF),
            pltpu.VMEM((2, half, 2, tok, hd), BF),
            pltpu.SMEM((18 * third,), jnp.int32),
            pltpu.SMEM((18 * third,), jnp.int32),
            pltpu.SMEM((heads * 4,), jnp.int32),
            pltpu.SMEM((heads * 4,), jnp.int32),
            pltpu.SMEM((heads * 4,), jnp.int32),
        ]
    )
    sems = ((2,), (2, 2, third), (2,), (2,), (1,), (2,), (2,), (2, 2, third), (2,), (2,), (3,), (2, 3), (2, 2))
    scratch += [dma(sem) for sem in sems]
    for _ in range(4):
        scratch += [pltpu.VMEM((2, tok, (half - third + 1 if k == 0 else 1) * hd), BF) for k in range(third)]
    scratch += [pltpu.VMEM((9, 2, tok, hd), BF) for _ in range(2 * third)]
    dq, dk, dv = pl.pallas_call(
        functools.partial(kernel, n_sh, n_sw, half, hd),
        out_shape=[pltpu.VMEM((tok, cols), BF)] * 3,
        in_specs=[hbm] * 7,
        out_specs=[vmem] * 3,
        scratch_shapes=scratch,
        compiler_params=pltpu.CompilerParams(
            collective_id=0, has_side_effects=True, vmem_limit_bytes=32 * 2**20
        ),
    )(flat(queries), flat(keys), flat(values), flat(attn_grad), flat(attn_out), flat(log_sum), place(window_dirs.T, pltpu.HBM))
    dq, dk, dv = pl.pallas_call(
        hand_out,
        out_shape=[jax.ShapeDtypeStruct((tok, cols), BF)] * 3,
        in_specs=[vmem] * 3,
        out_specs=[hbm] * 3,
        scratch_shapes=[dma((3,))],
    )(*(place(array, pltpu.VMEM) for array in (dq, dk, dv)))
    return tuple(array.reshape(shape) for array in (dq, dk, dv))


def solution(mesh):
    spec = P("tp", "sh", "sw", None)
    return jax.shard_map(
        functools.partial(local, mesh.shape["sh"], mesh.shape["sw"]),
        mesh=mesh,
        in_specs=(spec,) * 6 + (P(),),
        out_specs=(spec,) * 3,
        check_vma=False,
    )
```
